512 devices in a mesh: ctx: 64 (over x, y, core), head: 8 (over z).
Axes of the slice: x: 4, y: 8, z: 8, core: 2. Of those that a mesh axis runs over, the one named last changes fastest.
Arguments:
- queries: bfloat16 [32768, 4096], P('ctx', 'head'), may hold values from -200 to 200
- keys: bfloat16 [32768, 4096], P('ctx', 'head'), may hold values from -8 to 8
- values: bfloat16 [32768, 4096], P('ctx', 'head'), may hold values from -6 to 6
- out_grad: bfloat16 [32768, 4096], P(('ctx', 'head')), may hold values from -6 to 6
- context_keys: bfloat16 [8192, 4096], P('ctx', 'head'), may hold values from -6 to 6
- context_values: bfloat16 [8192, 4096], P('ctx', 'head'), may hold values from -6 to 6
- selected: int32 [32, 64, 3], P('head', 'ctx'), may hold values from 0 to 15, as said below
- doc_lengths: int32 [64], replicated, may hold values from 1 to 1024, 32768 in all
Outputs:
- attended: bfloat16 [32768, 4096], P(('ctx', 'head'))
- query_grad: bfloat16 [32768, 4096], P('ctx', 'head')
- key_grad: bfloat16 [32768, 4096], P('ctx', 'head')
- value_grad: bfloat16 [32768, 4096], P('ctx', 'head')
- context_key_grad: bfloat16 [8192, 4096], P('ctx', 'head')
- context_value_grad: bfloat16 [8192, 4096], P('ctx', 'head')
The draws below stay inside these ranges and needn't reach their ends.
Inputs may be any that keep to these rules, and one draw needn't show every extreme that they name: `selected`: the three entries of a row differ. Among the rows of one device (its 4 heads and 1 query blocks) no context block is named more than 1 times, and in every device's rows some block is named exactly 1 times.
All inputs are finite; a program needn't handle non-finite values.
Results may differ from the reference program's by a relative error of at most 0.0103.
The reference program's roundings to bfloat16 on the way (of `keys_all`, `values_all`, `weights_low` and `score_grads`) count: a program that leaves them out, or rounds other values in their place, can miss the bound.
Values may be sent and summed in bfloat16 or wider, within the bound.
No kernel may reach another device: no remote copies, remote signals or barrier semaphores. Data moves between devices by JAX's collectives and lax.ppermute only.
A program may use at most 128 MiB of HBM per device.

```python
import math
import jax
import jax.numpy as jnp
import numpy as np
from jax import lax

HEAD_DIM = 128
HEADS_DEV = 4
BLK = 512
NQ_DEV = 1
HEADS = 32
NQB = 64
QTOK = 32768
NCB = 16
CTOK = 8192
CAP = 1
NDOC = 64
DOC_MOST = 1024


def base_keys(key):
    shared = jax.random.normal(jax.random.fold_in(key, 501), (QTOK, HEADS, HEAD_DIM), jnp.float32)
    return jnp.clip(shared, -5.0, 5.0)


def draw_keys(key, part):
    shared = base_keys(key)
    return shared.reshape(QTOK, HEADS * HEAD_DIM).astype(jnp.bfloat16)


def draw_queries(key, part):
    fresh = jax.random.normal(jax.random.fold_in(key, 4), (QTOK, HEADS, HEAD_DIM), jnp.float32)
    fresh = jnp.clip(fresh, -6.0, 6.0)
    return fresh.reshape(QTOK, HEADS * HEAD_DIM).astype(jnp.bfloat16)


def draw_selected(key, part):
    key = jax.random.fold_in(key, 11)
    groups = HEADS // HEADS_DEV
    sources = NQB // NQ_DEV
    row_count = HEADS_DEV * NQ_DEV
    pick_total = 3 * row_count
    slot_total = NCB * CAP

    def one_device(device_key):
        favor_key, shuffle_key, row_key = jax.random.split(device_key, 3)
        favored = jax.random.randint(favor_key, (), 0, NCB)
        slot_ids = jnp.arange(slot_total, dtype=jnp.int32)
        shuffled = jax.random.permutation(shuffle_key, slot_total).astype(jnp.int32)
        ranking = jnp.where(slot_ids // CAP == favored, slot_ids % CAP - CAP, shuffled)
        taken_slots = jnp.argsort(ranking, stable=True)[:pick_total]
        marked = jnp.zeros((slot_total,), jnp.int32).at[taken_slots].set(1)
        ordered = jnp.argsort(1 - marked, stable=True)[:pick_total]
        owners = (ordered // CAP).astype(jnp.int32)
        row_order = jax.random.permutation(row_key, row_count).astype(jnp.int32)
        position = jnp.arange(pick_total, dtype=jnp.int32)
        row_table = jnp.zeros((row_count, 3), jnp.int32)
        row_table = row_table.at[row_order[position % row_count], position // row_count].set(owners)
        return row_table.reshape(HEADS_DEV, NQ_DEV, 3)
    device_keys = jax.random.split(key, groups * sources)
    tables = jax.vmap(one_device)(device_keys).reshape(groups, sources, HEADS_DEV, NQ_DEV, 3)
    return tables.transpose(0, 2, 1, 3, 4).reshape(HEADS, NQB, 3)


def block_levels(key, extent, cuts, smallest, top_value):
    factor_of, own = 1.0, jax.random.fold_in(key, 6)
    for dim, parts in cuts:
        steps = jnp.exp(jax.random.uniform(jax.random.fold_in(own, dim), (parts,), jnp.float32, smallest / len(cuts), top_value / len(cuts)))
        factor_of = factor_of * jnp.repeat(steps, extent[dim] // parts).reshape([-1 if axis == dim else 1 for axis in range(len(extent))])
    return factor_of


def length_profile(amount, total, bound, slope):
    portions = [(1 << 20) // math.isqrt(rank ** slope) + 1 for rank in range(2, amount + 1)]
    spare, holding = total - bound - (amount - 1), [1] * (amount - 1)
    while spare > 0:
        free = [i for i in range(amount - 1) if holding[i] < bound]
        mass, budget = sum([portions[i] for i in free]), spare
        for i in free:
            addition = min(bound - holding[i], max(1, budget * portions[i] // mass), spare)
            holding[i] = holding[i] + addition
            spare = spare - addition
    return np.array([bound] + holding)


def uneven_parts(key, amount, total, reach, skew):
    if amount == 2:
        one = jax.random.randint(key, (), max(1, total - reach), min(reach, total - 1) + 1)
        return jnp.stack([one, total - one])
    sizes = jnp.asarray(length_profile(amount, total, reach, skew), jnp.int32)
    pairs = (amount - 1) // 2
    source_of, taker = sizes[1:1 + 2 * pairs:2], sizes[2:2 + 2 * pairs:2]
    room = jnp.minimum(source_of - 1, reach - taker)
    moved = jax.random.randint(jax.random.fold_in(key, 1), (pairs,), 0, 1 << 20) % (room + 1)
    sizes = sizes.at[1:1 + 2 * pairs:2].set(source_of - moved).at[2:2 + 2 * pairs:2].set(taker + moved)
    return sizes[jax.random.permutation(jax.random.fold_in(key, 2), amount)]


def bell_draw(stream_key, extent, scale, reach, pieces=(), kind=jnp.bfloat16):
    loudness = block_levels(stream_key, extent, pieces, -0.22, 0.18) if pieces else 1.0
    array = jax.random.normal(stream_key, extent, jnp.float32) * scale * loudness
    return jnp.minimum(jnp.maximum(array, -reach), reach).astype(kind)


def setup_inputs(seed: int = 0) -> dict:
    streams_of = jax.random.split(jax.random.key(seed), 9)
    queries = draw_queries(jax.random.fold_in(streams_of[8], 71), 0)
    keys = draw_keys(jax.random.fold_in(streams_of[8], 71), 0)
    values = bell_draw(streams_of[2], (QTOK, HEADS * HEAD_DIM), 1.0, 6.0, ((0, 64), (1, 8)))
    out_grad = bell_draw(streams_of[3], (QTOK, HEADS * HEAD_DIM), 1.0, 6.0, ((0, 512),))
    context_keys = bell_draw(streams_of[4], (CTOK, HEADS * HEAD_DIM), 1.0, 6.0, ((0, 64), (1, 8)))
    context_values = bell_draw(streams_of[5], (CTOK, HEADS * HEAD_DIM), 1.0, 6.0, ((0, 64), (1, 8)))
    selected = draw_selected(jax.random.fold_in(streams_of[8], 71), 0)
    doc_lengths = uneven_parts(streams_of[7], NDOC, QTOK, DOC_MOST, 2).astype(jnp.int32)
    return {"queries": queries, "keys": keys, "values": values, "out_grad": out_grad, "context_keys": context_keys, "context_values": context_values, "selected": selected, "doc_lengths": doc_lengths}


def reference(queries, keys, values, out_grad, context_keys, context_values, selected, doc_lengths):
    score_scale = HEAD_DIM ** -0.5
    doc_ends = jnp.cumsum(doc_lengths)
    positions = jnp.arange(QTOK, dtype=jnp.int32)
    token_doc = jnp.sum((doc_ends[None, :] <= positions[:, None]).astype(jnp.int32), axis=1).reshape(NQB, BLK)
    inside = jnp.arange(BLK, dtype=jnp.int32)
    causal = inside[None, :] <= inside[:, None]
    query_blocks = queries.reshape(NQB, BLK, HEADS, HEAD_DIM)
    key_blocks = keys.reshape(NQB, BLK, HEADS, HEAD_DIM)
    value_blocks = values.reshape(NQB, BLK, HEADS, HEAD_DIM)
    grad_blocks = out_grad.reshape(NQB, BLK, HEADS, HEAD_DIM)
    context_k = context_keys.reshape(NCB, BLK, HEADS, HEAD_DIM)
    context_v = context_values.reshape(NCB, BLK, HEADS, HEAD_DIM)
    head_ids = jnp.arange(HEADS, dtype=jnp.int32)

    def advance(carry, block_index):
        grad_k, grad_v = carry
        chosen = selected[:, block_index]
        query_here = query_blocks[block_index].astype(jnp.float32)
        far_keys = context_k[chosen, :, head_ids[:, None], :]
        far_values = context_v[chosen, :, head_ids[:, None], :]
        keys_all = jnp.concatenate([key_blocks[block_index].transpose(1, 0, 2)[:, None], far_keys], axis=1)
        keys_all = keys_all.reshape(HEADS, 4 * BLK, HEAD_DIM).astype(jnp.float32)
        values_all = jnp.concatenate([value_blocks[block_index].transpose(1, 0, 2)[:, None], far_values], axis=1)
        values_all = values_all.reshape(HEADS, 4 * BLK, HEAD_DIM).astype(jnp.float32)
        scores = jnp.einsum('qhd,hkd->hqk', query_here, keys_all) * score_scale
        docs_here = token_doc[block_index]
        allowed = causal & (docs_here[None, :] == docs_here[:, None])
        near_part = jnp.where(allowed[None], scores[:, :, :BLK], -jnp.inf)
        scores = jnp.concatenate([near_part, scores[:, :, BLK:]], axis=-1)
        row_max = jnp.max(scores, axis=-1, keepdims=True)
        lifted = jnp.exp(scores - row_max)
        weights = lifted / jnp.sum(lifted, axis=-1, keepdims=True)
        weights_low = weights.astype(jnp.bfloat16)
        attended = jnp.einsum('hqk,hkd->qhd', weights_low.astype(jnp.float32), values_all).astype(jnp.bfloat16)
        grad_here = grad_blocks[block_index].astype(jnp.float32)
        weight_grads = jnp.einsum('qhd,hkd->hqk', grad_here, values_all)
        row_delta = jnp.sum(grad_here * attended.astype(jnp.float32), axis=-1).T[:, :, None]
        score_grads = (weights * (weight_grads - row_delta) * score_scale).astype(jnp.bfloat16)
        query_grad = jnp.einsum('hqk,hkd->qhd', score_grads.astype(jnp.float32), keys_all).astype(jnp.bfloat16)
        keys_grad_all = jnp.einsum('hqk,qhd->hkd', score_grads.astype(jnp.float32), query_here)
        values_grad_all = jnp.einsum('hqk,qhd->hkd', weights_low.astype(jnp.float32), grad_here)
        key_grad = keys_grad_all[:, :BLK].transpose(1, 0, 2).astype(jnp.bfloat16)
        value_grad = values_grad_all[:, :BLK].transpose(1, 0, 2).astype(jnp.bfloat16)
        far_kgrad = keys_grad_all[:, BLK:].reshape(HEADS, 3, BLK, HEAD_DIM)
        far_vgrad = values_grad_all[:, BLK:].reshape(HEADS, 3, BLK, HEAD_DIM)
        grad_k = grad_k.at[chosen, :, head_ids[:, None], :].add(far_kgrad)
        grad_v = grad_v.at[chosen, :, head_ids[:, None], :].add(far_vgrad)
        return (grad_k, grad_v), (attended, query_grad, key_grad, value_grad)

    zeros_grad = jnp.zeros((NCB, BLK, HEADS, HEAD_DIM), jnp.float32)
    (grad_k, grad_v), stacked = lax.scan(advance, (zeros_grad, zeros_grad), jnp.arange(NQB, dtype=jnp.int32))
    attended, query_grad, key_grad, value_grad = stacked
    flat_shape = (QTOK, HEADS * HEAD_DIM)
    context_shape = (CTOK, HEADS * HEAD_DIM)
    return (attended.reshape(flat_shape), query_grad.reshape(flat_shape), key_grad.reshape(flat_shape),
            value_grad.reshape(flat_shape), grad_k.astype(jnp.bfloat16).reshape(context_shape),
            grad_v.astype(jnp.bfloat16).reshape(context_shape))
```

```python
import jax
import jax.numpy as jnp
from jax import lax
from jax.experimental import pallas as pl
from jax.experimental.pallas import tpu as pltpu
from jax.sharding import PartitionSpec as P

NT = (((1,), (1,)), ((), ()))
NN = (((1,), (0,)), ((), ()))
VMEM_BYTES = 56 * 1024 * 1024


def dot(a, b, dims):
    return lax.dot_general(a, b, dims, preferred_element_type=jnp.float32)


def document_starts(lens_ref, base_ref, rows):
    position = base_ref[0] + lax.broadcasted_iota(jnp.int32, (1, rows), 1)

    def step(d, carry):
        total, start = carry
        total = total + lens_ref[d]
        return total, jnp.maximum(start, jnp.where(total <= position, total, 0))

    _, start = lax.fori_loop(
        0, lens_ref.shape[0], step, (jnp.int32(0), jnp.zeros((1, rows), jnp.int32))
    )
    return start - base_ref[0]


def masked(scores, start):
    key_at = lax.broadcasted_iota(jnp.int32, scores.shape, 0)
    query_at = lax.broadcasted_iota(jnp.int32, scores.shape, 1)
    return jnp.where((key_at <= query_at) & (key_at >= start), scores, -jnp.inf)


def pack_kernel(codes_ref, context_ref, out_ref):
    width = out_ref.shape[2]

    def step(d, carry):
        column = pl.multiple_of(jnp.maximum(codes_ref[d], 0) * width, width)
        out_ref[d] = context_ref[:, pl.ds(column, width)]
        return carry

    lax.fori_loop(0, out_ref.shape[0], step, 0)


def value_grad_kernel(
    sel_ref, lens_ref, base_ref, q_ref, k_ref, g_ref, far_k_ref,
    near_ref, far_ref, top_ref, inverse_ref, start_ref, scores_ref,
):
    head = pl.program_id(0)
    rows, width = q_ref.shape
    picks = scores_ref.shape[0] - 1
    scale = width ** (-0.5)

    @pl.when(head == 0)
    def _():
        start_ref[...] = document_starts(lens_ref, base_ref, rows)

    q = q_ref[...]
    near = masked(dot(k_ref[...], q, NT), start_ref[...])
    scores_ref[0] = near
    top = jnp.max(near, axis=0, keepdims=True)
    for j in range(picks):
        far = dot(far_k_ref[sel_ref[head * picks + j]], q, NT)
        scores_ref[j + 1] = far
        top = jnp.maximum(top, jnp.max(far, axis=0, keepdims=True))
    total = jnp.zeros((1, rows), jnp.float32)
    for j in range(picks + 1):
        lifted = jnp.exp((scores_ref[j] - top) * scale)
        scores_ref[j] = lifted
        total = total + jnp.sum(lifted, axis=0, keepdims=True)
    inverse = 1.0 / total
    top_ref[0] = top
    inverse_ref[0] = inverse
    g = g_ref[...]
    for j in range(picks + 1):
        low = (scores_ref[j] * inverse).astype(jnp.bfloat16)
        part = dot(low, g, NN).astype(jnp.bfloat16)
        if j == 0:
            near_ref[...] = part
        else:
            far_ref[sel_ref[head * picks + j - 1]] = part


def other_grads_kernel(
    sel_ref, lens_ref, base_ref, q_ref, k_ref, v_ref, g_ref, far_k_ref, far_v_ref, top_ref, inverse_ref,
    attended_ref, query_ref, near_ref, far_ref, start_ref, weights_ref,
):
    head = pl.program_id(0)
    rows, width = q_ref.shape
    picks = weights_ref.shape[0] - 1
    scale = width ** (-0.5)

    @pl.when(head == 0)
    def _():
        start_ref[...] = document_starts(lens_ref, base_ref, rows)

    def keys_of(j):
        return k_ref[...] if j == 0 else far_k_ref[sel_ref[head * picks + j - 1]]

    def values_of(j):
        return v_ref[...] if j == 0 else far_v_ref[sel_ref[head * picks + j - 1]]

    q = q_ref[...]
    g = g_ref[...]
    top = top_ref[0]
    inverse = inverse_ref[0]
    attended = jnp.zeros((width, rows), jnp.float32)
    for j in range(picks + 1):
        scores = dot(keys_of(j), q, NT)
        if j == 0:
            scores = masked(scores, start_ref[...])
        weights = jnp.exp((scores - top) * scale) * inverse
        weights_ref[j] = weights
        attended = attended + dot(values_of(j).T, weights.astype(jnp.bfloat16), NN)
    attended = attended.astype(jnp.bfloat16)
    attended_ref[...] = attended.T
    delta = jnp.sum(
        g.T.astype(jnp.float32) * attended.astype(jnp.float32), axis=0, keepdims=True
    )
    query_grad = jnp.zeros((width, rows), jnp.float32)
    for j in range(picks + 1):
        weight_grads = dot(values_of(j), g, NT)
        score_grads = (weights_ref[j] * (weight_grads - delta) * scale).astype(jnp.bfloat16)
        part = dot(score_grads, q, NN).astype(jnp.bfloat16)
        if j == 0:
            near_ref[...] = part
        else:
            far_ref[sel_ref[head * picks + j - 1]] = part
        query_grad = query_grad + dot(keys_of(j).T, score_grads, NN)
    query_ref[...] = query_grad.astype(jnp.bfloat16).T


def collect_kernel(codes_ref, terms_ref, out_ref, total_ref):
    step_at = pl.program_id(0)
    sources, rows, width = terms_ref.shape
    heads = total_ref.shape[0] - 1

    @pl.when(step_at == 0)
    def _():
        total_ref[...] = jnp.zeros_like(total_ref)

    def step(s, carry):
        code = codes_ref[step_at * sources + s]
        slot = jnp.where(code >= 0, code, heads)
        total_ref[slot] += terms_ref[s].astype(jnp.float32)
        return carry

    lax.fori_loop(0, sources, step, 0)

    @pl.when(step_at == pl.num_programs(0) - 1)
    def _():
        for h in range(heads):
            out_ref[:, h * width : (h + 1) * width] = total_ref[h].astype(out_ref.dtype)


def pack(codes, context, owners, width):
    rows = context.shape[0]
    return pl.pallas_call(
        pack_kernel,
        out_shape=jax.ShapeDtypeStruct((owners, rows, width), context.dtype),
        grid_spec=pltpu.PrefetchScalarGridSpec(
            num_scalar_prefetch=1,
            grid=(1,),
            in_specs=[pl.BlockSpec(context.shape, lambda i, *_: (0, 0))],
            out_specs=pl.BlockSpec((owners, rows, width), lambda i, *_: (0, 0, 0)),
        ),
        compiler_params=pltpu.CompilerParams(vmem_limit_bytes=VMEM_BYTES),
    )(codes, context)


def collect(codes, terms, heads):
    owners, rows, width = terms.shape
    steps = 4
    return pl.pallas_call(
        collect_kernel,
        out_shape=jax.ShapeDtypeStruct((rows, heads * width), terms.dtype),
        grid_spec=pltpu.PrefetchScalarGridSpec(
            num_scalar_prefetch=1,
            grid=(steps,),
            in_specs=[pl.BlockSpec((owners // steps, rows, width), lambda i, *_: (i, 0, 0))],
            out_specs=pl.BlockSpec((rows, heads * width), lambda i, *_: (0, 0)),
            scratch_shapes=[pltpu.VMEM((heads + 1, rows, width), jnp.float32)],
        ),
        compiler_params=pltpu.CompilerParams(vmem_limit_bytes=VMEM_BYTES),
    )(codes, terms)


def on_device(queries, keys, values, out_grad, context_keys, context_values, selected, doc_lengths):
    heads, _, picks = selected.shape
    rows = queries.shape[0]
    width = queries.shape[1] // heads
    piece_rows = context_keys.shape[0]
    pieces = rows // piece_rows
    owners = lax.axis_size("ctx")
    blocks = owners // pieces
    base = (lax.axis_index("ctx") * rows).astype(jnp.int32).reshape(1)
    flat = selected.reshape(-1)

    head_of = jnp.arange(heads * picks, dtype=jnp.int32) // picks
    hits = flat[None, :] == jnp.arange(blocks, dtype=jnp.int32)[:, None]
    wanted = jnp.max(jnp.where(hits, head_of[None, :], -1), axis=1)
    wanted = jnp.broadcast_to(wanted[:, None, None], (blocks, pieces, 128)).reshape(owners, 128)
    codes = lax.all_to_all(wanted, "ctx", split_axis=0, concat_axis=0, tiled=True)[:, 0]

    def exchange(tiles):
        return lax.all_to_all(tiles, "ctx", split_axis=0, concat_axis=0, tiled=True)

    far_keys = exchange(pack(codes, context_keys, owners, width)).reshape(blocks, rows, width)
    far_values = exchange(pack(codes, context_values, owners, width)).reshape(blocks, rows, width)
    grads = lax.all_to_all(out_grad, "head", split_axis=1, concat_axis=0, tiled=True)

    by_head = pl.BlockSpec((rows, width), lambda h, *_: (0, h))
    all_far = pl.BlockSpec((blocks, rows, width), lambda h, *_: (0, 0, 0))
    by_stat = pl.BlockSpec((1, 1, rows), lambda h, *_: (h, 0, 0))
    near_shape = jax.ShapeDtypeStruct(queries.shape, jnp.bfloat16)
    far_shape = jax.ShapeDtypeStruct((blocks, rows, width), jnp.bfloat16)
    stat_shape = jax.ShapeDtypeStruct((heads, 1, rows), jnp.float32)
    scratch = [pltpu.VMEM((1, rows), jnp.int32), pltpu.VMEM((picks + 1, rows, rows), jnp.float32)]
    tile_flops = 2 * rows * rows * width * (picks + 1) * heads
    value_grad, far_value_grads, top, inverse = pl.pallas_call(
        value_grad_kernel,
        out_shape=(near_shape, far_shape, stat_shape, stat_shape),
        grid_spec=pltpu.PrefetchScalarGridSpec(
            num_scalar_prefetch=3,
            grid=(heads,),
            in_specs=[by_head, by_head, by_head, all_far],
            out_specs=[by_head, all_far, by_stat, by_stat],
            scratch_shapes=scratch,
        ),
        compiler_params=pltpu.CompilerParams(vmem_limit_bytes=VMEM_BYTES),
        cost_estimate=pl.CostEstimate(
            flops=2 * tile_flops, bytes_accessed=8 << 20, transcendentals=heads * 4 * rows * rows
        ),
    )(flat, doc_lengths, base, queries, keys, grads, far_keys)
    value_terms = exchange(far_value_grads.reshape(owners, piece_rows, width))

    attended, query_grad, key_grad, far_key_grads = pl.pallas_call(
        other_grads_kernel,
        out_shape=(near_shape, near_shape, near_shape, far_shape),
        grid_spec=pltpu.PrefetchScalarGridSpec(
            num_scalar_prefetch=3,
            grid=(heads,),
            in_specs=[by_head, by_head, by_head, by_head, all_far, all_far, by_stat, by_stat],
            out_specs=[by_head, by_head, by_head, all_far],
            scratch_shapes=scratch,
        ),
        compiler_params=pltpu.CompilerParams(vmem_limit_bytes=VMEM_BYTES),
        cost_estimate=pl.CostEstimate(
            flops=5 * tile_flops, bytes_accessed=8 << 20, transcendentals=heads * 4 * rows * rows
        ),
    )(flat, doc_lengths, base, queries, keys, values, grads, far_keys, far_values, top, inverse)
    key_terms = exchange(far_key_grads.reshape(owners, piece_rows, width))

    output_rows = lax.all_to_all(attended, "head", split_axis=0, concat_axis=1, tiled=True)
    context_value_grad = collect(codes, value_terms, heads)
    context_key_grad = collect(codes, key_terms, heads)
    return output_rows, query_grad, key_grad, value_grad, context_key_grad, context_value_grad


def solution(mesh):
    split = P("ctx", "head")
    rows = P(("ctx", "head"), None)
    return jax.shard_map(
        on_device,
        mesh=mesh,
        in_specs=(split, split, split, rows, split, split, P("head", "ctx", None), P()),
        out_specs=(rows, split, split, split, split, split),
        check_vma=False,
    )
```

```python
import jax
import jax.numpy as jnp
from jax import lax
from jax.experimental import pallas as pl
from jax.experimental.pallas import tpu as pltpu
from jax.sharding import PartitionSpec as P

NT = (((1,), (1,)), ((), ()))
NN = (((1,), (0,)), ((), ()))
VMEM_BYTES = 56 * 1024 * 1024


def dot(a, b, dims):
    return lax.dot_general(a, b, dims, preferred_element_type=jnp.float32)


def document_starts(lens_ref, base_ref, rows):
    position = base_ref[0] + lax.broadcasted_iota(jnp.int32, (1, rows), 1)

    def step(d, carry):
        total, start = carry
        total = total + lens_ref[d]
        return total, jnp.maximum(start, jnp.where(total <= position, total, 0))

    _, start = lax.fori_loop(
        0, lens_ref.shape[0], step, (jnp.int32(0), jnp.zeros((1, rows), jnp.int32))
    )
    return start - base_ref[0]


def masked(scores, start):
    key_at = lax.broadcasted_iota(jnp.int32, scores.shape, 0)
    query_at = lax.broadcasted_iota(jnp.int32, scores.shape, 1)
    return jnp.where((key_at <= query_at) & (key_at >= start), scores, -jnp.inf)


def pack_kernel(codes_ref, context_ref, out_ref):
    count, _, width = out_ref.shape
    first = pl.program_id(0) * count

    def step(d, carry):
        column = pl.multiple_of(jnp.maximum(codes_ref[first + d], 0) * width, width)
        out_ref[d] = context_ref[:, pl.ds(column, width)]
        return carry

    lax.fori_loop(0, count, step, 0, unroll=4)


def in_token_order(me, shares, out_ref):
    count = len(shares)
    rows = shares[0].shape[0]
    for distance, share in enumerate(shares):
        source = lax.rem(me + count - distance, count)
        out_ref[pl.ds(pl.multiple_of(source * rows, rows), rows), :] = share[...]


def assemble_kernel(me_ref, *refs):
    *shares, out_ref = refs
    count = len(shares)
    width = shares[0].shape[1]
    for distance, share in enumerate(shares):
        source = lax.rem(me_ref[0] + count - distance, count)
        out_ref[:, pl.ds(pl.multiple_of(source * width, width), width)] = share[...]


def gate_kernel(kept_ref, after_ref, out_ref):
    pass


def value_grad_kernel(
    sel_ref, lens_ref, base_ref, q_ref, k_ref, k1_ref, k2_ref, k3_ref, *refs,
):
    *shares, near_ref, far_ref, top_ref, inverse_ref, start_ref, scores_ref, g_ref = refs
    far_k = (k1_ref, k2_ref, k3_ref)
    head = pl.program_id(0)
    rows, width = q_ref.shape
    picks = scores_ref.shape[0] - 1
    scale = width ** (-0.5)

    @pl.when(head == 0)
    def _():
        start_ref[...] = document_starts(lens_ref, base_ref, rows)

    q = q_ref[...]
    near = masked(dot(k_ref[...], q, NT), start_ref[...])
    scores_ref[0] = near
    top = jnp.max(near, axis=0, keepdims=True)
    for j in range(picks):
        far = dot(far_k[j][...], q, NT)
        scores_ref[j + 1] = far
        top = jnp.maximum(top, jnp.max(far, axis=0, keepdims=True))
    total = jnp.zeros((1, rows), jnp.float32)
    for j in range(picks + 1):
        lifted = jnp.exp((scores_ref[j] - top) * scale)
        scores_ref[j] = lifted
        total = total + jnp.sum(lifted, axis=0, keepdims=True)
    inverse = 1.0 / total
    top_ref[0] = top
    inverse_ref[0] = inverse
    in_token_order(base_ref[1], shares, g_ref)
    g = g_ref[...]
    for j in range(picks + 1):
        low = (scores_ref[j] * inverse).astype(jnp.bfloat16)
        part = dot(low, g, NN).astype(jnp.bfloat16)
        if j == 0:
            near_ref[...] = part
        else:
            far_ref[sel_ref[head * picks + j - 1]] = part


def other_grads_kernel(
    sel_ref, lens_ref, base_ref, q_ref, k_ref, v_ref,
    k1_ref, k2_ref, k3_ref, v1_ref, v2_ref, v3_ref, top_ref, inverse_ref, *refs,
):
    *shares, attended_ref, query_ref, near_ref, far_ref, start_ref, weights_ref, g_ref = refs
    far_k, far_v = (k1_ref, k2_ref, k3_ref), (v1_ref, v2_ref, v3_ref)
    head = pl.program_id(0)
    rows, width = q_ref.shape
    picks = weights_ref.shape[0] - 1
    scale = width ** (-0.5)

    @pl.when(head == 0)
    def _():
        start_ref[...] = document_starts(lens_ref, base_ref, rows)

    def keys_of(j):
        return k_ref[...] if j == 0 else far_k[j - 1][...]

    def values_of(j):
        return v_ref[...] if j == 0 else far_v[j - 1][0]

    in_token_order(base_ref[1], shares, g_ref)
    q = q_ref[...]
    g = g_ref[...]
    top = top_ref[0]
    inverse = inverse_ref[0]
    attended = jnp.zeros((width, rows), jnp.float32)
    for j in range(picks + 1):
        scores = dot(keys_of(j), q, NT)
        if j == 0:
            scores = masked(scores, start_ref[...])
        weights = jnp.exp((scores - top) * scale) * inverse
        weights_ref[j] = weights
        attended = attended + dot(values_of(j).T, weights.astype(jnp.bfloat16), NN)
    attended = attended.astype(jnp.bfloat16)
    attended_ref[...] = attended.T
    delta = jnp.sum(
        g.T.astype(jnp.float32) * attended.astype(jnp.float32), axis=0, keepdims=True
    )
    query_grad = jnp.zeros((width, rows), jnp.float32)
    for j in range(picks + 1):
        weight_grads = dot(values_of(j), g, NT)
        score_grads = (weights_ref[j] * (weight_grads - delta) * scale).astype(jnp.bfloat16)
        part = dot(score_grads, q, NN).astype(jnp.bfloat16)
        if j == 0:
            near_ref[...] = part
        else:
            far_ref[sel_ref[head * picks + j - 1]] = part
        query_grad = query_grad + dot(keys_of(j).T, score_grads, NN)
    query_ref[...] = query_grad.astype(jnp.bfloat16).T


def collect_kernel(codes_ref, terms_ref, out_ref, total_ref):
    step_at = pl.program_id(0)
    sources, rows, width = terms_ref.shape
    heads = total_ref.shape[0] - 1

    @pl.when(step_at == 0)
    def _():
        total_ref[...] = jnp.zeros_like(total_ref)

    def step(s, carry):
        code = codes_ref[step_at * sources + s]
        slot = jnp.where(code >= 0, code, heads)
        total_ref[slot] += terms_ref[s].astype(jnp.float32)
        return carry

    lax.fori_loop(0, sources, step, 0)

    @pl.when(step_at == pl.num_programs(0) - 1)
    def _():
        for h in range(heads):
            out_ref[:, h * width : (h + 1) * width] = total_ref[h].astype(out_ref.dtype)


def pack(codes, context, owners, width):
    rows = context.shape[0]
    steps = 4
    return pl.pallas_call(
        pack_kernel,
        out_shape=jax.ShapeDtypeStruct((owners, rows, width), context.dtype),
        grid_spec=pltpu.PrefetchScalarGridSpec(
            num_scalar_prefetch=1,
            grid=(steps,),
            in_specs=[pl.BlockSpec(context.shape, lambda i, *_: (0, 0))],
            out_specs=pl.BlockSpec((owners // steps, rows, width), lambda i, *_: (i, 0, 0)),
        ),
        compiler_params=pltpu.CompilerParams(vmem_limit_bytes=VMEM_BYTES),
    )(codes, context)


def collect(codes, terms, heads):
    owners, rows, width = terms.shape
    steps = 4
    return pl.pallas_call(
        collect_kernel,
        out_shape=jax.ShapeDtypeStruct((rows, heads * width), terms.dtype),
        grid_spec=pltpu.PrefetchScalarGridSpec(
            num_scalar_prefetch=1,
            grid=(steps,),
            in_specs=[pl.BlockSpec((owners // steps, rows, width), lambda i, *_: (i, 0, 0))],
            out_specs=pl.BlockSpec((rows, heads * width), lambda i, *_: (0, 0)),
            scratch_shapes=[pltpu.VMEM((heads + 1, rows, width), jnp.float32)],
        ),
        compiler_params=pltpu.CompilerParams(vmem_limit_bytes=VMEM_BYTES),
    )(codes, terms)


def shifted(parts, count):
    return [parts[0]] + [
        lax.ppermute(parts[d], "head", [(i, (i + d) % count) for i in range(count)])
        for d in range(1, count)
    ]


def gate(kept, after):
    return pl.pallas_call(
        gate_kernel,
        out_shape=jax.ShapeDtypeStruct(kept.shape, kept.dtype),
        in_specs=[pl.BlockSpec(memory_space=pl.ANY)] * 2,
        out_specs=pl.BlockSpec(memory_space=pl.ANY),
        input_output_aliases={0: 0},
    )(kept, after)


def on_device(queries, keys, values, out_grad, context_keys, context_values, selected, doc_lengths):
    heads, _, picks = selected.shape
    rows = queries.shape[0]
    width = queries.shape[1] // heads
    piece_rows = context_keys.shape[0]
    pieces = rows // piece_rows
    owners = lax.axis_size("ctx")
    blocks = owners // pieces
    gathered_keys = lax.all_gather(context_keys, "ctx", axis=0, tiled=True)
    count = lax.axis_size("head")
    me = lax.axis_index("head").astype(jnp.int32)
    share_rows = rows // count
    grads = shifted(
        [
            lax.dynamic_slice_in_dim(
                out_grad, lax.rem(me + d, count) * heads * width, heads * width, 1
            )
            for d in range(count)
        ],
        count,
    )
    base = jnp.stack([lax.axis_index("ctx").astype(jnp.int32) * rows, me])
    flat = selected.reshape(-1)

    head_of = jnp.arange(heads * picks, dtype=jnp.int32) // picks
    hits = flat[None, :] == jnp.arange(blocks, dtype=jnp.int32)[:, None]
    wanted = jnp.max(jnp.where(hits, head_of[None, :], -1), axis=1)
    wanted = jnp.broadcast_to(wanted[:, None, None], (blocks, pieces, 128)).reshape(owners, 128)
    codes = lax.all_to_all(wanted, "ctx", split_axis=0, concat_axis=0, tiled=True)[:, 0]

    def exchange(tiles):
        return lax.all_to_all(tiles, "ctx", split_axis=0, concat_axis=0, tiled=True)

    far_values = exchange(pack(codes, context_values, owners, width)).reshape(blocks, rows, width)

    by_head = pl.BlockSpec((rows, width), lambda h, *_: (0, h))
    all_far = pl.BlockSpec((blocks, rows, width), lambda h, *_: (0, 0, 0))
    far_key = [
        pl.BlockSpec((rows, width), lambda h, sel, *_, j=j: (sel[h * picks + j], h))
        for j in range(picks)
    ]
    far_value = [
        pl.BlockSpec((1, rows, width), lambda h, sel, *_, j=j: (sel[h * picks + j], 0, 0))
        for j in range(picks)
    ]
    shares = [pl.BlockSpec((share_rows, width), lambda h, *_: (0, h))] * count
    by_stat = pl.BlockSpec((1, 1, rows), lambda h, *_: (h, 0, 0))
    near_shape = jax.ShapeDtypeStruct(queries.shape, jnp.bfloat16)
    far_shape = jax.ShapeDtypeStruct((blocks, rows, width), jnp.bfloat16)
    stat_shape = jax.ShapeDtypeStruct((heads, 1, rows), jnp.float32)
    scratch = [
        pltpu.VMEM((1, rows), jnp.int32),
        pltpu.VMEM((picks + 1, rows, rows), jnp.float32),
        pltpu.VMEM((rows, width), jnp.bfloat16),
    ]
    tile_flops = 2 * rows * rows * width * (picks + 1) * heads
    value_grad, far_value_grads, top, inverse = pl.pallas_call(
        value_grad_kernel,
        out_shape=(near_shape, far_shape, stat_shape, stat_shape),
        grid_spec=pltpu.PrefetchScalarGridSpec(
            num_scalar_prefetch=3,
            grid=(heads,),
            in_specs=[by_head, by_head, *far_key, *shares],
            out_specs=[by_head, all_far, by_stat, by_stat],
            scratch_shapes=scratch,
        ),
        compiler_params=pltpu.CompilerParams(vmem_limit_bytes=VMEM_BYTES),
        cost_estimate=pl.CostEstimate(
            flops=2 * tile_flops, bytes_accessed=8 << 20, transcendentals=heads * 4 * rows * rows
        ),
    )(flat, doc_lengths, base, queries, keys, *[gathered_keys] * picks, *grads)
    value_terms = exchange(far_value_grads.reshape(owners, piece_rows, width))

    attended, query_grad, key_grad, far_key_grads = pl.pallas_call(
        other_grads_kernel,
        out_shape=(near_shape, near_shape, near_shape, far_shape),
        grid_spec=pltpu.PrefetchScalarGridSpec(
            num_scalar_prefetch=3,
            grid=(heads,),
            in_specs=[by_head, by_head, by_head, *far_key, *far_value, by_stat, by_stat, *shares],
            out_specs=[by_head, by_head, by_head, all_far],
            scratch_shapes=scratch,
        ),
        compiler_params=pltpu.CompilerParams(vmem_limit_bytes=VMEM_BYTES),
        cost_estimate=pl.CostEstimate(
            flops=5 * tile_flops, bytes_accessed=8 << 20, transcendentals=heads * 4 * rows * rows
        ),
    )(
        flat, doc_lengths, base, queries, keys, values,
        *[gathered_keys] * picks, *[far_values] * picks, top, inverse, *grads,
    )
    key_terms = exchange(gate(far_key_grads.reshape(owners, piece_rows, width), value_terms))

    output_parts = shifted(
        [
            lax.dynamic_slice_in_dim(attended, lax.rem(me + d, count) * share_rows, share_rows, 0)
            for d in range(count)
        ],
        count,
    )
    output_rows = pl.pallas_call(
        assemble_kernel,
        out_shape=jax.ShapeDtypeStruct((share_rows, count * heads * width), jnp.bfloat16),
        in_specs=[pl.BlockSpec(memory_space=pltpu.SMEM)]
        + [pl.BlockSpec(memory_space=pltpu.VMEM)] * count,
        out_specs=pl.BlockSpec(memory_space=pltpu.VMEM),
    )(me.reshape(1), *output_parts)
    context_value_grad = collect(codes, value_terms, heads)
    context_key_grad = collect(codes, key_terms, heads)
    return output_rows, query_grad, key_grad, value_grad, context_key_grad, context_value_grad


def solution(mesh):
    split = P("ctx", "head")
    rows = P(("ctx", "head"), None)
    return jax.shard_map(
        on_device,
        mesh=mesh,
        in_specs=(split, split, split, rows, split, split, P("head", "ctx", None), P()),
        out_specs=(rows, split, split, split, split, split),
        check_vma=False,
    )
```

```python
import jax
import jax.numpy as jnp
from jax import lax
from jax.experimental import pallas as pl
from jax.experimental.pallas import tpu as pltpu
from jax.sharding import Mesh
from jax.sharding import PartitionSpec as P

NT = (((1,), (1,)), ((), ()))
NN = (((1,), (0,)), ((), ()))
SIZE_X, SIZE_Y, CORES = 4, 8, 2
CTX = ("x", "y", "core")
VMEM_BYTES = 56 * 1024 * 1024


def dot(a, b, dims):
    return lax.dot_general(a, b, dims, preferred_element_type=jnp.float32)


def document_starts(lens_ref, base_ref, rows):
    position = base_ref[0] + lax.broadcasted_iota(jnp.int32, (1, rows), 1)

    def step(d, carry):
        total, start = carry
        total = total + lens_ref[d]
        return total, jnp.maximum(start, jnp.where(total <= position, total, 0))

    _, start = lax.fori_loop(
        0, lens_ref.shape[0], step, (jnp.int32(0), jnp.zeros((1, rows), jnp.int32))
    )
    return start - base_ref[0]


def masked(scores, start):
    key_at = lax.broadcasted_iota(jnp.int32, scores.shape, 0)
    query_at = lax.broadcasted_iota(jnp.int32, scores.shape, 1)
    return jnp.where((key_at <= query_at) & (key_at >= start), scores, -jnp.inf)


def pack_kernel(codes_ref, context_ref, *refs):
    out_ref = refs[-1]
    count, rows, width = out_ref.shape
    first = pl.program_id(0) * count
    groups = context_ref.shape[0] // rows
    for j in range(count):
        column = pl.multiple_of(jnp.maximum(codes_ref[first + j], 0) * width, width)
        start = (j % groups) * rows
        out_ref[j] = context_ref[start : start + rows, pl.ds(column, width)]


def in_token_order(me, shares, out_ref):
    count = len(shares)
    rows = shares[0].shape[0]
    for distance, share in enumerate(shares):
        source = lax.rem(me + count - distance, count)
        out_ref[pl.ds(pl.multiple_of(source * rows, rows), rows), :] = share[...]


def tile_of(parts):
    rows = parts[0].shape[-2] // CORES
    return jnp.concatenate(
        [part[0, 0, p * rows : (p + 1) * rows] for p in range(CORES) for part in parts], axis=0
    )


def assemble_kernel(me_ref, *refs):
    *shares, out_ref = refs
    count = len(shares)
    width = shares[0].shape[1]
    for distance, share in enumerate(shares):
        source = lax.rem(me_ref[0] + count - distance, count)
        out_ref[:, pl.ds(pl.multiple_of(source * width, width), width)] = share[...]


def gate_kernel(kept_ref, after_ref, out_ref):
    pass


def value_grad_kernel(
    sel_ref, lens_ref, base_ref, q_ref, k_ref, k1_ref, k2_ref, k3_ref, *refs,
):
    *shares, near_ref, far_ref, top_ref, inverse_ref, start_ref, scores_ref, g_ref = refs
    far_k = (k1_ref, k2_ref, k3_ref)
    head = pl.program_id(0)
    rows, width = q_ref.shape
    picks = scores_ref.shape[0] - 1
    scale = width ** (-0.5)

    @pl.when(head == 0)
    def _():
        start_ref[...] = document_starts(lens_ref, base_ref, rows)

    q = q_ref[...]
    near = masked(dot(k_ref[...], q, NT), start_ref[...])
    scores_ref[0] = near
    top = jnp.max(near, axis=0, keepdims=True)
    for j in range(picks):
        far = dot(far_k[j][0], q, NT)
        scores_ref[j + 1] = far
        top = jnp.maximum(top, jnp.max(far, axis=0, keepdims=True))
    total = jnp.zeros((1, rows), jnp.float32)
    for j in range(picks + 1):
        lifted = jnp.exp((scores_ref[j] - top) * scale)
        scores_ref[j] = lifted
        total = total + jnp.sum(lifted, axis=0, keepdims=True)
    inverse = 1.0 / total
    top_ref[0] = top
    inverse_ref[0] = inverse
    in_token_order(base_ref[1], shares, g_ref)
    g = g_ref[...]
    for j in range(picks + 1):
        low = (scores_ref[j] * inverse).astype(jnp.bfloat16)
        part = dot(low, g, NN).astype(jnp.bfloat16)
        if j == 0:
            near_ref[...] = part
        else:
            far_ref[sel_ref[head * picks + j - 1]] = part


def other_grads_kernel(
    sel_ref, lens_ref, base_ref, q_ref, k_ref, v_ref,
    k1_ref, k2_ref, k3_ref, *refs,
):
    *far_v, top_ref, inverse_ref = refs[:8]
    *shares, attended_ref, query_ref, near_ref, far_ref, start_ref, weights_ref, g_ref = refs[8:]
    far_k = (k1_ref, k2_ref, k3_ref)
    head = pl.program_id(0)
    rows, width = q_ref.shape
    picks = weights_ref.shape[0] - 1
    scale = width ** (-0.5)

    @pl.when(head == 0)
    def _():
        start_ref[...] = document_starts(lens_ref, base_ref, rows)

    def keys_of(j):
        return k_ref[...] if j == 0 else far_k[j - 1][0]

    def values_of(j):
        return v_ref[...] if j == 0 else tile_of(far_v[2 * j - 2 : 2 * j])

    in_token_order(base_ref[1], shares, g_ref)
    q = q_ref[...]
    g = g_ref[...]
    top = top_ref[0]
    inverse = inverse_ref[0]
    attended = jnp.zeros((width, rows), jnp.float32)
    for j in range(picks + 1):
        scores = dot(keys_of(j), q, NT)
        if j == 0:
            scores = masked(scores, start_ref[...])
        weights = jnp.exp((scores - top) * scale) * inverse
        weights_ref[j] = weights
        attended = attended + dot(values_of(j).T, weights.astype(jnp.bfloat16), NN)
    attended = attended.astype(jnp.bfloat16)
    attended_ref[...] = attended.T
    delta = jnp.sum(
        g.T.astype(jnp.float32) * attended.astype(jnp.float32), axis=0, keepdims=True
    )
    query_grad = jnp.zeros((width, rows), jnp.float32)
    for j in range(picks + 1):
        weight_grads = dot(values_of(j), g, NT)
        score_grads = (weights_ref[j] * (weight_grads - delta) * scale).astype(jnp.bfloat16)
        part = dot(score_grads, q, NN).astype(jnp.bfloat16)
        if j == 0:
            near_ref[...] = part
        else:
            far_ref[sel_ref[head * picks + j - 1]] = part
        query_grad = query_grad + dot(keys_of(j).T, score_grads, NN)
    query_ref[...] = query_grad.astype(jnp.bfloat16).T


def collect_kernel(codes_ref, terms_ref, out_ref, total_ref):
    step_at = pl.program_id(0)
    sources, rows, width = terms_ref.shape
    heads = total_ref.shape[0] - 1

    @pl.when(step_at == 0)
    def _():
        total_ref[...] = jnp.zeros_like(total_ref)

    def step(s, carry):
        code = codes_ref[step_at * sources + s]
        slot = jnp.where(code >= 0, code, heads)
        total_ref[slot] += terms_ref[s].astype(jnp.float32)
        return carry

    lax.fori_loop(0, sources, step, 0)

    @pl.when(step_at == pl.num_programs(0) - 1)
    def _():
        for h in range(heads):
            out_ref[:, h * width : (h + 1) * width] = total_ref[h].astype(out_ref.dtype)


def pack(codes, context, groups, width):
    slots = codes.shape[0]
    rows = context.shape[0] // groups
    steps = 4
    return pl.pallas_call(
        pack_kernel,
        out_shape=jax.ShapeDtypeStruct((slots, rows, width), context.dtype),
        grid_spec=pltpu.PrefetchScalarGridSpec(
            num_scalar_prefetch=1,
            grid=(steps,),
            in_specs=[pl.BlockSpec(context.shape, lambda i, *_: (0, 0))],
            out_specs=pl.BlockSpec((slots // steps, rows, width), lambda i, *_: (i, 0, 0)),
        ),
        compiler_params=pltpu.CompilerParams(vmem_limit_bytes=VMEM_BYTES),
    )(codes, context)


def collect(codes, terms, heads):
    owners, rows, width = terms.shape
    steps = 4
    return pl.pallas_call(
        collect_kernel,
        out_shape=jax.ShapeDtypeStruct((rows, heads * width), terms.dtype),
        grid_spec=pltpu.PrefetchScalarGridSpec(
            num_scalar_prefetch=1,
            grid=(steps,),
            in_specs=[pl.BlockSpec((owners // steps, rows, width), lambda i, *_: (i, 0, 0))],
            out_specs=pl.BlockSpec((rows, heads * width), lambda i, *_: (0, 0)),
            scratch_shapes=[pltpu.VMEM((heads + 1, rows, width), jnp.float32)],
        ),
        compiler_params=pltpu.CompilerParams(vmem_limit_bytes=VMEM_BYTES),
    )(codes, terms)


def shifted(parts, count):
    return [parts[0]] + [
        lax.ppermute(parts[d], "head", [(i, (i + d) % count) for i in range(count)])
        for d in range(1, count)
    ]


def gate(kept, after):
    return pl.pallas_call(
        gate_kernel,
        out_shape=jax.ShapeDtypeStruct(kept.shape, kept.dtype),
        in_specs=[pl.BlockSpec(memory_space=pl.ANY)] * 2,
        out_specs=pl.BlockSpec(memory_space=pl.ANY),
        input_output_aliases={0: 0},
    )(kept, after)


def on_device(queries, keys, values, out_grad, context_keys, context_values, selected, doc_lengths):
    heads, _, picks = selected.shape
    rows = queries.shape[0]
    width = queries.shape[1] // heads
    piece_rows = context_keys.shape[0]
    pieces = rows // piece_rows
    owners = lax.axis_size(CTX)
    blocks = owners // pieces
    my_x, my_y = lax.axis_index("x"), lax.axis_index("y")
    my_piece = lax.axis_index(CTX).astype(jnp.int32)
    column_values = lax.all_gather(context_values, "y", axis=0, tiled=True)
    count = lax.axis_size("head")
    me = lax.axis_index("head").astype(jnp.int32)
    share_rows = rows // count
    grads = shifted(
        [
            lax.dynamic_slice_in_dim(
                out_grad, lax.rem(me + d, count) * heads * width, heads * width, 1
            )
            for d in range(count)
        ],
        count,
    )
    flat = selected.reshape(-1)

    head_of = jnp.arange(heads * picks, dtype=jnp.int32) // picks
    hits = flat[None, :] == jnp.arange(blocks, dtype=jnp.int32)[:, None]
    wanted = jnp.max(jnp.where(hits, head_of[None, :], -1), axis=1)
    wanted = jnp.broadcast_to(jnp.pad(wanted, (0, 128 - blocks)), (owners, 128))
    codes = lax.all_to_all(wanted, CTX, split_axis=0, concat_axis=0, tiled=True)
    piece_codes = lax.dynamic_slice_in_dim(codes, my_piece // pieces, 1, 1)[:, 0]
    own_x = blocks // SIZE_X
    peers = SIZE_X * CORES
    me_row = (my_x * CORES + lax.axis_index("core")).astype(jnp.int32)
    base = jnp.stack([my_piece * rows, me, me_row])
    row_codes = lax.dynamic_slice(
        codes.reshape(SIZE_X, SIZE_Y, CORES, 128),
        (0, my_y, 0, my_x * own_x),
        (SIZE_X, 1, CORES, own_x),
    ).reshape(peers, own_x)
    row_codes = jnp.concatenate([row_codes, row_codes])
    row_codes = lax.dynamic_slice_in_dim(row_codes, me_row, peers, 0).reshape(-1)

    def to_holders(tiles):
        tiles = tiles.reshape(owners, piece_rows, width)
        return lax.all_to_all(tiles, CTX, split_axis=0, concat_axis=0, tiled=True)

    far_keys = to_holders(pack(piece_codes, context_keys, 1, width)).reshape(blocks, rows, width)
    sent = pack(row_codes, column_values, own_x, width).reshape(peers, own_x, rows // CORES, width)
    far_values = [sent[0]] + [
        lax.ppermute(sent[d], ("x", "core"), [(i, (i + d) % peers) for i in range(peers)])
        for d in range(1, peers)
    ]
    far_values = jnp.stack(far_values)

    by_head = pl.BlockSpec((rows, width), lambda h, *_: (0, h))
    all_far = pl.BlockSpec((blocks, rows, width), lambda h, *_: (0, 0, 0))
    far_key = [
        pl.BlockSpec((1, rows, width), lambda h, sel, *_, j=j: (sel[h * picks + j], 0, 0))
        for j in range(picks)
    ]

    def value_at(j, c):
        def index(h, sel, lens, base):
            block = sel[h * picks + j]
            source = (block // own_x) * CORES + c
            return (lax.rem(base[2] + peers - source, peers), lax.rem(block, own_x), 0, 0)

        return pl.BlockSpec((1, 1, rows // CORES, width), index)

    far_value = [value_at(j, c) for j in range(picks) for c in range(CORES)]
    shares = [pl.BlockSpec((share_rows, width), lambda h, *_: (0, h))] * count
    by_stat = pl.BlockSpec((1, 1, rows), lambda h, *_: (h, 0, 0))
    near_shape = jax.ShapeDtypeStruct(queries.shape, jnp.bfloat16)
    far_shape = jax.ShapeDtypeStruct((blocks, rows, width), jnp.bfloat16)
    stat_shape = jax.ShapeDtypeStruct((heads, 1, rows), jnp.float32)
    scratch = [
        pltpu.VMEM((1, rows), jnp.int32),
        pltpu.VMEM((picks + 1, rows, rows), jnp.float32),
        pltpu.VMEM((rows, width), jnp.bfloat16),
    ]
    tile_flops = 2 * rows * rows * width * (picks + 1) * heads
    value_grad, far_value_grads, top, inverse = pl.pallas_call(
        value_grad_kernel,
        out_shape=(near_shape, far_shape, stat_shape, stat_shape),
        grid_spec=pltpu.PrefetchScalarGridSpec(
            num_scalar_prefetch=3,
            grid=(heads,),
            in_specs=[by_head, by_head, *far_key, *shares],
            out_specs=[by_head, all_far, by_stat, by_stat],
            scratch_shapes=scratch,
        ),
        compiler_params=pltpu.CompilerParams(vmem_limit_bytes=VMEM_BYTES),
        cost_estimate=pl.CostEstimate(
            flops=2 * tile_flops, bytes_accessed=8 << 20, transcendentals=heads * 4 * rows * rows
        ),
    )(flat, doc_lengths, base, queries, keys, *[far_keys] * picks, *grads)
    value_terms = to_holders(far_value_grads)

    attended, query_grad, key_grad, far_key_grads = pl.pallas_call(
        other_grads_kernel,
        out_shape=(near_shape, near_shape, near_shape, far_shape),
        grid_spec=pltpu.PrefetchScalarGridSpec(
            num_scalar_prefetch=3,
            grid=(heads,),
            in_specs=[by_head, by_head, by_head, *far_key, *far_value, by_stat, by_stat, *shares],
            out_specs=[by_head, by_head, by_head, all_far],
            scratch_shapes=scratch,
        ),
        compiler_params=pltpu.CompilerParams(vmem_limit_bytes=VMEM_BYTES),
        cost_estimate=pl.CostEstimate(
            flops=5 * tile_flops, bytes_accessed=8 << 20, transcendentals=heads * 4 * rows * rows
        ),
    )(
        flat, doc_lengths, base, queries, keys, values,
        *[far_keys] * picks, *[far_values] * len(far_value), top, inverse, *grads,
    )
    key_terms = to_holders(gate(far_key_grads, value_terms))

    output_parts = shifted(
        [
            lax.dynamic_slice_in_dim(attended, lax.rem(me + d, count) * share_rows, share_rows, 0)
            for d in range(count)
        ],
        count,
    )
    output_rows = pl.pallas_call(
        assemble_kernel,
        out_shape=jax.ShapeDtypeStruct((share_rows, count * heads * width), jnp.bfloat16),
        in_specs=[pl.BlockSpec(memory_space=pltpu.SMEM)]
        + [pl.BlockSpec(memory_space=pltpu.VMEM)] * count,
        out_specs=pl.BlockSpec(memory_space=pltpu.VMEM),
    )(me.reshape(1), *output_parts)
    context_value_grad = collect(piece_codes, value_terms, heads)
    context_key_grad = collect(piece_codes, key_terms, heads)
    return output_rows, query_grad, key_grad, value_grad, context_key_grad, context_value_grad


def solution(mesh):
    devices = mesh.devices.reshape(SIZE_X, SIZE_Y, CORES, -1)
    split = P(CTX, "head")
    rows = P((*CTX, "head"), None)
    return jax.shard_map(
        on_device,
        mesh=Mesh(devices, (*CTX, "head")),
        in_specs=(split, split, split, rows, split, split, P("head", CTX, None), P()),
        out_specs=(rows, split, split, split, split, split),
        check_vma=False,
    )
```

```python
import jax
import jax.numpy as jnp
from jax import lax
from jax.experimental import pallas as pl
from jax.experimental.pallas import tpu as pltpu
from jax.sharding import Mesh
from jax.sharding import PartitionSpec as P

NT = (((1,), (1,)), ((), ()))
NN = (((1,), (0,)), ((), ()))
SIZE_X, SIZE_Y, CORES = 4, 8, 2
CTX = ("x", "y", "core")
VMEM_BYTES = 56 * 1024 * 1024


def dot(a, b, dims):
    return lax.dot_general(a, b, dims, preferred_element_type=jnp.float32)


def document_starts(lens_ref, base_ref, rows):
    position = base_ref[0] + lax.broadcasted_iota(jnp.int32, (1, rows), 1)

    def step(d, carry):
        total, start = carry
        total = total + lens_ref[d]
        return total, jnp.maximum(start, jnp.where(total <= position, total, 0))

    _, start = lax.fori_loop(
        0, lens_ref.shape[0], step, (jnp.int32(0), jnp.zeros((1, rows), jnp.int32))
    )
    return start - base_ref[0]


def masked(scores, start):
    key_at = lax.broadcasted_iota(jnp.int32, scores.shape, 0)
    query_at = lax.broadcasted_iota(jnp.int32, scores.shape, 1)
    return jnp.where((key_at <= query_at) & (key_at >= start), scores, -jnp.inf)


def pack_kernel(codes_ref, context_ref, *refs):
    out_ref = refs[-1]
    count, rows, width = out_ref.shape
    first = pl.program_id(0) * count
    groups = context_ref.shape[0] // rows
    for j in range(count):
        column = pl.multiple_of(jnp.maximum(codes_ref[first + j], 0) * width, width)
        start = (j % groups) * rows
        out_ref[j] = context_ref[start : start + rows, pl.ds(column, width)]


def in_token_order(me, shares, out_ref):
    count = len(shares)
    rows = shares[0].shape[0]
    for distance, share in enumerate(shares):
        source = lax.rem(me + count - distance, count)
        out_ref[pl.ds(pl.multiple_of(source * rows, rows), rows), :] = share[...]


def tile_of(ref):
    return ref[...].reshape(-1, ref.shape[-1])


def store_pieces(out_ref, block, part):
    count, rows = out_ref.shape[1:3]
    for c in range(CORES):
        for p in range(count // CORES):
            at = (c * (count // CORES) + p) * rows
            out_ref[block, p * CORES + c] = part[at : at + rows]


def assemble_kernel(me_ref, *refs):
    *shares, out_ref = refs
    count = len(shares)
    width = shares[0].shape[1]
    for distance, share in enumerate(shares):
        source = lax.rem(me_ref[0] + count - distance, count)
        out_ref[:, pl.ds(pl.multiple_of(source * width, width), width)] = share[...]


def gate_kernel(kept_ref, after_ref, out_ref):
    pass


def value_grad_kernel(
    sel_ref, lens_ref, base_ref, q_ref, k_ref, k1_ref, k2_ref, k3_ref, *refs,
):
    *shares, near_ref, far_ref, top_ref, inverse_ref, start_ref, scores_ref, g_ref = refs
    far_k = (k1_ref, k2_ref, k3_ref)
    head = pl.program_id(0)
    rows, width = q_ref.shape
    picks = scores_ref.shape[0] - 1
    scale = width ** (-0.5)

    @pl.when(head == 0)
    def _():
        start_ref[...] = document_starts(lens_ref, base_ref, rows)

    q = q_ref[...]
    near = masked(dot(k_ref[...], q, NT), start_ref[...])
    scores_ref[0] = near
    top = jnp.max(near, axis=0, keepdims=True)
    for j in range(picks):
        far = dot(tile_of(far_k[j]), q, NT)
        scores_ref[j + 1] = far
        top = jnp.maximum(top, jnp.max(far, axis=0, keepdims=True))
    total = jnp.zeros((1, rows), jnp.float32)
    for j in range(picks + 1):
        lifted = jnp.exp((scores_ref[j] - top) * scale)
        scores_ref[j] = lifted
        total = total + jnp.sum(lifted, axis=0, keepdims=True)
    inverse = 1.0 / total
    top_ref[0] = top
    inverse_ref[0] = inverse
    in_token_order(base_ref[1], shares, g_ref)
    g = g_ref[...]
    for j in range(picks + 1):
        low = (scores_ref[j] * inverse).astype(jnp.bfloat16)
        part = dot(low, g, NN).astype(jnp.bfloat16)
        if j == 0:
            near_ref[...] = part
        else:
            block = sel_ref[head * picks + j - 1]
            own_x, rows_core = far_ref.shape[2:4]
            for c in range(CORES):
                far_ref[block // own_x, c, lax.rem(block, own_x)] = part[
                    c * rows_core : (c + 1) * rows_core
                ]


def other_grads_kernel(
    sel_ref, lens_ref, base_ref, q_ref, k_ref, v_ref,
    k1_ref, k2_ref, k3_ref, v1_ref, v2_ref, v3_ref, top_ref, inverse_ref, *refs,
):
    *shares, attended_ref, query_ref, near_ref, far_ref, start_ref, weights_ref, g_ref = refs
    far_k, far_v = (k1_ref, k2_ref, k3_ref), (v1_ref, v2_ref, v3_ref)
    head = pl.program_id(0)
    rows, width = q_ref.shape
    picks = weights_ref.shape[0] - 1
    scale = width ** (-0.5)

    @pl.when(head == 0)
    def _():
        start_ref[...] = document_starts(lens_ref, base_ref, rows)

    def keys_of(j):
        return k_ref[...] if j == 0 else tile_of(far_k[j - 1])

    def values_of(j):
        return v_ref[...] if j == 0 else tile_of(far_v[j - 1])

    in_token_order(base_ref[1], shares, g_ref)
    q = q_ref[...]
    g = g_ref[...]
    top = top_ref[0]
    inverse = inverse_ref[0]
    attended = jnp.zeros((width, rows), jnp.float32)
    for j in range(picks + 1):
        scores = dot(keys_of(j), q, NT)
        if j == 0:
            scores = masked(scores, start_ref[...])
        weights = jnp.exp((scores - top) * scale) * inverse
        weights_ref[j] = weights
        attended = attended + dot(values_of(j).T, weights.astype(jnp.bfloat16), NN)
    attended = attended.astype(jnp.bfloat16)
    attended_ref[...] = attended.T
    delta = jnp.sum(
        g.T.astype(jnp.float32) * attended.astype(jnp.float32), axis=0, keepdims=True
    )
    query_grad = jnp.zeros((width, rows), jnp.float32)
    for j in range(picks + 1):
        weight_grads = dot(values_of(j), g, NT)
        score_grads = (weights_ref[j] * (weight_grads - delta) * scale).astype(jnp.bfloat16)
        part = dot(score_grads, q, NN).astype(jnp.bfloat16)
        if j == 0:
            near_ref[...] = part
        else:
            store_pieces(far_ref, sel_ref[head * picks + j - 1], part)
        query_grad = query_grad + dot(keys_of(j).T, score_grads, NN)
    query_ref[...] = query_grad.astype(jnp.bfloat16).T


def collect_kernel(codes_ref, terms_ref, out_ref, total_ref):
    step_at = pl.program_id(0)
    sources, rows, width = terms_ref.shape
    heads = total_ref.shape[0] - 1

    @pl.when(step_at == 0)
    def _():
        total_ref[...] = jnp.zeros_like(total_ref)

    def step(s, carry):
        code = codes_ref[step_at * sources + s]
        slot = jnp.where(code >= 0, code, heads)
        total_ref[slot] += terms_ref[s].astype(jnp.float32)
        return carry

    lax.fori_loop(0, sources, step, 0)

    @pl.when(step_at == pl.num_programs(0) - 1)
    def _():
        for h in range(heads):
            out_ref[:, h * width : (h + 1) * width] = total_ref[h].astype(out_ref.dtype)


def pack(codes, context, half, groups, width, *after):
    slots = codes.shape[0]
    rows, columns = context.shape[0], context.shape[1] // 2
    steps = 4
    return pl.pallas_call(
        pack_kernel,
        out_shape=jax.ShapeDtypeStruct((slots, rows // groups, width), context.dtype),
        grid_spec=pltpu.PrefetchScalarGridSpec(
            num_scalar_prefetch=1,
            grid=(steps,),
            in_specs=[pl.BlockSpec((rows, columns), lambda i, *_: (0, half))]
            + [pl.BlockSpec(memory_space=pl.ANY)] * len(after),
            out_specs=pl.BlockSpec((slots // steps, rows // groups, width), lambda i, *_: (i, 0, 0)),
        ),
        compiler_params=pltpu.CompilerParams(vmem_limit_bytes=VMEM_BYTES),
    )(codes, context, *after)


def row_sum_kernel(codes_ref, terms_ref, out_ref, total_ref):
    block = pl.program_id(0)
    sources, _, rows, width = terms_ref.shape
    heads = total_ref.shape[0] - 1
    total_ref[...] = jnp.zeros_like(total_ref)

    def step(s, carry):
        code = codes_ref[s * pl.num_programs(0) + block]
        slot = jnp.where(code >= 0, code, heads)
        total_ref[slot] += terms_ref[s, 0].astype(jnp.float32)
        return carry

    lax.fori_loop(0, sources, step, 0)
    for h in range(heads):
        out_ref[:, h * width : (h + 1) * width] = total_ref[h].astype(out_ref.dtype)


def row_sum(codes, terms, heads):
    sources, blocks, rows, width = terms.shape
    return pl.pallas_call(
        row_sum_kernel,
        out_shape=jax.ShapeDtypeStruct((blocks * rows, heads * width), terms.dtype),
        grid_spec=pltpu.PrefetchScalarGridSpec(
            num_scalar_prefetch=1,
            grid=(blocks,),
            in_specs=[pl.BlockSpec((sources, 1, rows, width), lambda i, *_: (0, i, 0, 0))],
            out_specs=pl.BlockSpec((rows, heads * width), lambda i, *_: (i, 0)),
            scratch_shapes=[pltpu.VMEM((heads + 1, rows, width), jnp.float32)],
        ),
        compiler_params=pltpu.CompilerParams(vmem_limit_bytes=VMEM_BYTES),
    )(codes, terms)


def collect(codes, terms, heads):
    owners, rows, width = terms.shape
    steps = 4
    return pl.pallas_call(
        collect_kernel,
        out_shape=jax.ShapeDtypeStruct((rows, heads * width), terms.dtype),
        grid_spec=pltpu.PrefetchScalarGridSpec(
            num_scalar_prefetch=1,
            grid=(steps,),
            in_specs=[pl.BlockSpec((owners // steps, rows, width), lambda i, *_: (i, 0, 0))],
            out_specs=pl.BlockSpec((rows, heads * width), lambda i, *_: (0, 0)),
            scratch_shapes=[pltpu.VMEM((heads + 1, rows, width), jnp.float32)],
        ),
        compiler_params=pltpu.CompilerParams(vmem_limit_bytes=VMEM_BYTES),
    )(codes, terms)


def shifted(parts, count):
    return [parts[0]] + [
        lax.ppermute(parts[d], "head", [(i, (i + d) % count) for i in range(count)])
        for d in range(1, count)
    ]


def gate(kept, after):
    return pl.pallas_call(
        gate_kernel,
        out_shape=jax.ShapeDtypeStruct(kept.shape, kept.dtype),
        in_specs=[pl.BlockSpec(memory_space=pl.ANY)] * 2,
        out_specs=pl.BlockSpec(memory_space=pl.ANY),
        input_output_aliases={0: 0},
    )(kept, after)


def on_device(queries, keys, values, out_grad, context_keys, context_values, selected, doc_lengths):
    heads, _, picks = selected.shape
    rows = queries.shape[0]
    width = queries.shape[1] // heads
    piece_rows = context_keys.shape[0]
    pieces = rows // piece_rows
    owners = lax.axis_size(CTX)
    blocks = owners // pieces
    my_x, my_y = lax.axis_index("x"), lax.axis_index("y")
    my_piece = lax.axis_index(CTX).astype(jnp.int32)
    column = lax.all_gather(
        jnp.concatenate([context_keys, context_values], axis=1), "y", axis=0, tiled=True
    )
    count = lax.axis_size("head")
    me = lax.axis_index("head").astype(jnp.int32)
    share_rows = rows // count
    grads = shifted(
        [
            lax.dynamic_slice_in_dim(
                out_grad, lax.rem(me + d, count) * heads * width, heads * width, 1
            )
            for d in range(count)
        ],
        count,
    )
    base = jnp.stack([my_piece * rows, me])
    flat = selected.reshape(-1)

    head_of = jnp.arange(heads * picks, dtype=jnp.int32) // picks
    hits = flat[None, :] == jnp.arange(blocks, dtype=jnp.int32)[:, None]
    wanted = jnp.max(jnp.where(hits, head_of[None, :], -1), axis=1)
    wanted = jnp.broadcast_to(jnp.pad(wanted, (0, 128 - blocks)), (owners, 128))
    codes = lax.all_to_all(wanted, CTX, split_axis=0, concat_axis=0, tiled=True)
    piece_codes = lax.dynamic_slice_in_dim(codes, my_piece // pieces, 1, 1)[:, 0]
    own_x = blocks // SIZE_X
    row_codes = lax.dynamic_slice(
        codes.reshape(SIZE_X, SIZE_Y, CORES, 128),
        (0, my_y, 0, my_x * own_x),
        (SIZE_X, 1, CORES, own_x),
    ).reshape(-1)
    peers = SIZE_X * CORES

    row_shape = (SIZE_X, CORES, own_x, rows // CORES, width)

    def along_row(tiles):
        tiles = tiles.reshape(peers, own_x, rows // CORES, width)
        received = lax.all_to_all(tiles, ("x", "core"), split_axis=0, concat_axis=0, tiled=True)
        return received.reshape(row_shape)

    def to_holders(tiles):
        tiles = tiles.reshape(owners, piece_rows, width)
        return lax.all_to_all(tiles, CTX, split_axis=0, concat_axis=0, tiled=True)

    early = count - 1
    far_keys = along_row(pack(row_codes, column, 0, own_x, width, *grads[1:early]))
    far_values = along_row(pack(row_codes, column, 1, own_x, width, *grads[early:]))

    by_head = pl.BlockSpec((rows, width), lambda h, *_: (0, h))
    all_rows = pl.BlockSpec(row_shape, lambda h, *_: (0, 0, 0, 0, 0))
    all_far = pl.BlockSpec((blocks, pieces, piece_rows, width), lambda h, *_: (0, 0, 0, 0))
    far = [
        pl.BlockSpec(
            (1, CORES, 1, rows // CORES, width),
            lambda h, sel, *_, j=j: (sel[h * picks + j] // own_x, 0, sel[h * picks + j] % own_x, 0, 0),
        )
        for j in range(picks)
    ]
    shares = [pl.BlockSpec((share_rows, width), lambda h, *_: (0, h))] * count
    by_stat = pl.BlockSpec((1, 1, rows), lambda h, *_: (h, 0, 0))
    near_shape = jax.ShapeDtypeStruct(queries.shape, jnp.bfloat16)
    far_shape = jax.ShapeDtypeStruct((blocks, pieces, piece_rows, width), jnp.bfloat16)
    stat_shape = jax.ShapeDtypeStruct((heads, 1, rows), jnp.float32)
    scratch = [
        pltpu.VMEM((1, rows), jnp.int32),
        pltpu.VMEM((picks + 1, rows, rows), jnp.float32),
        pltpu.VMEM((rows, width), jnp.bfloat16),
    ]
    tile_flops = 2 * rows * rows * width * (picks + 1) * heads
    value_grad, far_value_grads, top, inverse = pl.pallas_call(
        value_grad_kernel,
        out_shape=(
            near_shape,
            jax.ShapeDtypeStruct(row_shape, jnp.bfloat16),
            stat_shape,
            stat_shape,
        ),
        grid_spec=pltpu.PrefetchScalarGridSpec(
            num_scalar_prefetch=3,
            grid=(heads,),
            in_specs=[by_head, by_head, *far, *shares],
            out_specs=[by_head, all_rows, by_stat, by_stat],
            scratch_shapes=scratch,
        ),
        compiler_params=pltpu.CompilerParams(vmem_limit_bytes=VMEM_BYTES),
        cost_estimate=pl.CostEstimate(
            flops=2 * tile_flops, bytes_accessed=8 << 20, transcendentals=heads * 4 * rows * rows
        ),
    )(flat, doc_lengths, base, queries, keys, *[far_keys] * picks, *grads)
    value_terms = along_row(gate(far_value_grads, far_values))
    value_sums = row_sum(row_codes, value_terms.reshape(peers, *row_shape[2:]), heads)
    context_value_grad = lax.psum_scatter(value_sums, "y", scatter_dimension=0, tiled=True)

    attended, query_grad, key_grad, far_key_grads = pl.pallas_call(
        other_grads_kernel,
        out_shape=(near_shape, near_shape, near_shape, far_shape),
        grid_spec=pltpu.PrefetchScalarGridSpec(
            num_scalar_prefetch=3,
            grid=(heads,),
            in_specs=[by_head, by_head, by_head, *far, *far, by_stat, by_stat, *shares],
            out_specs=[by_head, by_head, by_head, all_far],
            scratch_shapes=scratch,
        ),
        compiler_params=pltpu.CompilerParams(vmem_limit_bytes=VMEM_BYTES),
        cost_estimate=pl.CostEstimate(
            flops=5 * tile_flops, bytes_accessed=8 << 20, transcendentals=heads * 4 * rows * rows
        ),
    )(
        flat, doc_lengths, base, queries, keys, values,
        *[far_keys] * picks, *[far_values] * picks, top, inverse, *grads,
    )
    key_terms = to_holders(gate(far_key_grads, value_terms))

    output_parts = shifted(
        [
            lax.dynamic_slice_in_dim(attended, lax.rem(me + d, count) * share_rows, share_rows, 0)
            for d in range(count)
        ],
        count,
    )
    output_rows = pl.pallas_call(
        assemble_kernel,
        out_shape=jax.ShapeDtypeStruct((share_rows, count * heads * width), jnp.bfloat16),
        in_specs=[pl.BlockSpec(memory_space=pltpu.SMEM)]
        + [pl.BlockSpec(memory_space=pltpu.VMEM)] * count,
        out_specs=pl.BlockSpec(memory_space=pltpu.VMEM),
    )(me.reshape(1), *output_parts)
    context_key_grad = collect(piece_codes, key_terms, heads)
    return output_rows, query_grad, key_grad, value_grad, context_key_grad, context_value_grad


def solution(mesh):
    devices = mesh.devices.reshape(SIZE_X, SIZE_Y, CORES, -1)
    split = P(CTX, "head")
    rows = P((*CTX, "head"), None)
    return jax.shard_map(
        on_device,
        mesh=Mesh(devices, (*CTX, "head")),
        in_specs=(split, split, split, rows, split, split, P("head", CTX, None), P()),
        out_specs=(rows, split, split, split, split, split),
        check_vma=False,
    )
```

```python
import jax
import jax.numpy as jnp
from jax import lax
from jax.experimental import pallas as pl
from jax.experimental.pallas import tpu as pltpu
from jax.sharding import Mesh
from jax.sharding import PartitionSpec as P

NT = (((1,), (1,)), ((), ()))
NN = (((1,), (0,)), ((), ()))
SIZE_X, SIZE_Y, CORES = 4, 8, 2
CTX = ("x", "y", "core")
MIB = 1024 * 1024


def dot(a, b, dims):
    return lax.dot_general(a, b, dims, preferred_element_type=jnp.float32)


def document_starts(lens_ref, base_ref, rows):
    position = base_ref[0] + lax.broadcasted_iota(jnp.int32, (1, rows), 1)

    def step(d, carry):
        total, start = carry
        total = total + lens_ref[d]
        return total, jnp.maximum(start, jnp.where(total <= position, total, 0))

    _, start = lax.fori_loop(
        0, lens_ref.shape[0], step, (jnp.int32(0), jnp.zeros((1, rows), jnp.int32))
    )
    return start - base_ref[0]


def masked(scores, start):
    key_at = lax.broadcasted_iota(jnp.int32, scores.shape, 0)
    query_at = lax.broadcasted_iota(jnp.int32, scores.shape, 1)
    return jnp.where((key_at <= query_at) & (key_at >= start), scores, -jnp.inf)


def pack_kernel(codes_ref, context_ref, *refs):
    out_ref = refs[-1]
    count, rows, width = out_ref.shape
    first = pl.program_id(0) * count
    groups = context_ref.shape[0] // rows
    for j in range(count):
        column = pl.multiple_of(jnp.maximum(codes_ref[first + j], 0) * width, width)
        start = (j % groups) * rows
        out_ref[j] = context_ref[start : start + rows, pl.ds(column, width)]


def in_token_order(me, shares, out_ref):
    count = len(shares)
    rows = shares[0].shape[0]
    for distance, share in enumerate(shares):
        source = lax.rem(me + count - distance, count)
        out_ref[pl.ds(pl.multiple_of(source * rows, rows), rows), :] = share[...]


def tile_of(ref):
    return ref[...].reshape(-1, ref.shape[-1])


def store_halves(out_ref, block, part):
    own_x, rows = out_ref.shape[2:4]
    for c in range(CORES):
        out_ref[block // own_x, c, lax.rem(block, own_x)] = part[c * rows : (c + 1) * rows]


def assemble_kernel(me_ref, *refs):
    *shares, out_ref = refs
    count = len(shares)
    width = shares[0].shape[1]
    for distance, share in enumerate(shares):
        source = lax.rem(me_ref[0] + count - distance, count)
        out_ref[:, pl.ds(pl.multiple_of(source * width, width), width)] = share[...]


def gate_kernel(kept_ref, after_ref, out_ref):
    pass


def value_grad_kernel(
    sel_ref, lens_ref, base_ref, q_ref, k_ref, k1_ref, k2_ref, k3_ref, *refs,
):
    *shares, near_ref, far_ref, top_ref, inverse_ref, start_ref, scores_ref, g_ref = refs
    far_k = (k1_ref, k2_ref, k3_ref)
    head = pl.program_id(0)
    rows, width = q_ref.shape
    picks = scores_ref.shape[0] - 1
    scale = width ** (-0.5)

    @pl.when(head == 0)
    def _():
        start_ref[...] = document_starts(lens_ref, base_ref, rows)

    q = q_ref[...]
    near = masked(dot(k_ref[...], q, NT), start_ref[...])
    scores_ref[0] = near
    top = jnp.max(near, axis=0, keepdims=True)
    for j in range(picks):
        far = dot(tile_of(far_k[j]), q, NT)
        scores_ref[j + 1] = far
        top = jnp.maximum(top, jnp.max(far, axis=0, keepdims=True))
    total = jnp.zeros((1, rows), jnp.float32)
    for j in range(picks + 1):
        lifted = jnp.exp((scores_ref[j] - top) * scale)
        scores_ref[j] = lifted
        total = total + jnp.sum(lifted, axis=0, keepdims=True)
    inverse = 1.0 / total
    top_ref[0] = top
    inverse_ref[0] = inverse
    in_token_order(base_ref[1], shares, g_ref)
    g = g_ref[...]
    for j in range(picks + 1):
        low = (scores_ref[j] * inverse).astype(jnp.bfloat16)
        part = dot(low, g, NN).astype(jnp.bfloat16)
        if j == 0:
            near_ref[...] = part
        else:
            store_halves(far_ref, sel_ref[head * picks + j - 1], part)


def other_grads_kernel(
    sel_ref, lens_ref, base_ref, q_ref, k_ref, v_ref,
    k1_ref, k2_ref, k3_ref, v1_ref, v2_ref, v3_ref, top_ref, inverse_ref, *refs,
):
    *shares, attended_ref, query_ref, near_ref, far_ref, start_ref, weights_ref, g_ref = refs
    far_k, far_v = (k1_ref, k2_ref, k3_ref), (v1_ref, v2_ref, v3_ref)
    head = pl.program_id(0)
    rows, width = q_ref.shape
    picks = weights_ref.shape[0] - 1
    scale = width ** (-0.5)

    @pl.when(head == 0)
    def _():
        start_ref[...] = document_starts(lens_ref, base_ref, rows)

    def keys_of(j):
        return k_ref[...] if j == 0 else tile_of(far_k[j - 1])

    def values_of(j):
        return v_ref[...] if j == 0 else tile_of(far_v[j - 1])

    in_token_order(base_ref[1], shares, g_ref)
    q = q_ref[...]
    g = g_ref[...]
    top = top_ref[0]
    inverse = inverse_ref[0]
    attended = jnp.zeros((width, rows), jnp.float32)
    for j in range(picks + 1):
        scores = dot(keys_of(j), q, NT)
        if j == 0:
            scores = masked(scores, start_ref[...])
        weights = jnp.exp((scores - top) * scale) * inverse
        weights_ref[j] = weights
        attended = attended + dot(values_of(j).T, weights.astype(jnp.bfloat16), NN)
    attended = attended.astype(jnp.bfloat16)
    attended_ref[...] = attended.T
    delta = jnp.sum(
        g.T.astype(jnp.float32) * attended.astype(jnp.float32), axis=0, keepdims=True
    )
    query_grad = jnp.zeros((width, rows), jnp.float32)
    for j in range(picks + 1):
        weight_grads = dot(values_of(j), g, NT)
        score_grads = (weights_ref[j] * (weight_grads - delta) * scale).astype(jnp.bfloat16)
        part = dot(score_grads, q, NN).astype(jnp.bfloat16)
        if j == 0:
            near_ref[...] = part
        else:
            store_halves(far_ref, sel_ref[head * picks + j - 1], part)
        query_grad = query_grad + dot(keys_of(j).T, score_grads, NN)
    query_ref[...] = query_grad.astype(jnp.bfloat16).T


def pack(codes, context, half, groups, width, *after):
    slots = codes.shape[0]
    rows, columns = context.shape[0], context.shape[1] // 2
    steps = 4
    return pl.pallas_call(
        pack_kernel,
        out_shape=jax.ShapeDtypeStruct((slots, rows // groups, width), context.dtype),
        grid_spec=pltpu.PrefetchScalarGridSpec(
            num_scalar_prefetch=1,
            grid=(steps,),
            in_specs=[pl.BlockSpec((rows, columns), lambda i, *_: (0, half))]
            + [pl.BlockSpec(memory_space=pl.ANY)] * len(after),
            out_specs=pl.BlockSpec((slots // steps, rows // groups, width), lambda i, *_: (i, 0, 0)),
        ),
        compiler_params=pltpu.CompilerParams(vmem_limit_bytes=60 * MIB),
    )(codes, context, *after)


def row_sum_kernel(codes_ref, terms_ref, *refs):
    out_ref, total_ref = refs[-2:]
    block = pl.program_id(0)
    sources, _, rows, width = terms_ref.shape
    heads = total_ref.shape[0] - 1
    total_ref[...] = jnp.zeros_like(total_ref)

    def step(s, carry):
        code = codes_ref[s * pl.num_programs(0) + block]
        slot = jnp.where(code >= 0, code, heads)
        total_ref[slot] += terms_ref[s, 0].astype(jnp.float32)
        return carry

    lax.fori_loop(0, sources, step, 0)
    for h in range(heads):
        out_ref[:, h * width : (h + 1) * width] = total_ref[h].astype(out_ref.dtype)


def row_sum(codes, terms, heads, *after):
    sources, blocks, rows, width = terms.shape
    return pl.pallas_call(
        row_sum_kernel,
        out_shape=jax.ShapeDtypeStruct((blocks * rows, heads * width), terms.dtype),
        grid_spec=pltpu.PrefetchScalarGridSpec(
            num_scalar_prefetch=1,
            grid=(blocks,),
            in_specs=[pl.BlockSpec((sources, 1, rows, width), lambda i, *_: (0, i, 0, 0))]
            + [pl.BlockSpec(memory_space=pl.ANY)] * len(after),
            out_specs=pl.BlockSpec((rows, heads * width), lambda i, *_: (i, 0)),
            scratch_shapes=[pltpu.VMEM((heads + 1, rows, width), jnp.float32)],
        ),
        compiler_params=pltpu.CompilerParams(vmem_limit_bytes=6 * MIB),
    )(codes, terms, *after)


def shifted(parts, count):
    return [parts[0]] + [
        lax.ppermute(parts[d], "head", [(i, (i + d) % count) for i in range(count)])
        for d in range(1, count)
    ]


def gate(kept, after):
    return pl.pallas_call(
        gate_kernel,
        out_shape=jax.ShapeDtypeStruct(kept.shape, kept.dtype),
        in_specs=[pl.BlockSpec(memory_space=pl.ANY)] * 2,
        out_specs=pl.BlockSpec(memory_space=pl.ANY),
        input_output_aliases={0: 0},
    )(kept, after)


def on_device(queries, keys, values, out_grad, context_keys, context_values, selected, doc_lengths):
    heads, _, picks = selected.shape
    rows = queries.shape[0]
    width = queries.shape[1] // heads
    piece_rows = context_keys.shape[0]
    pieces = rows // piece_rows
    owners = lax.axis_size(CTX)
    blocks = owners // pieces
    my_x, my_y = lax.axis_index("x"), lax.axis_index("y")
    my_piece = lax.axis_index(CTX).astype(jnp.int32)
    column = lax.all_gather(
        jnp.concatenate([context_keys, context_values], axis=1), "y", axis=0, tiled=True
    )
    count = lax.axis_size("head")
    me = lax.axis_index("head").astype(jnp.int32)
    share_rows = rows // count
    grads = shifted(
        [
            lax.dynamic_slice_in_dim(
                out_grad, lax.rem(me + d, count) * heads * width, heads * width, 1
            )
            for d in range(count)
        ],
        count,
    )
    base = jnp.stack([my_piece * rows, me])
    flat = selected.reshape(-1)

    head_of = jnp.arange(heads * picks, dtype=jnp.int32) // picks
    hits = flat[None, :] == jnp.arange(blocks, dtype=jnp.int32)[:, None]
    wanted = jnp.max(jnp.where(hits, head_of[None, :], -1), axis=1)
    wanted = jnp.broadcast_to(jnp.pad(wanted, (0, 128 - blocks)), (owners, 128))
    codes = lax.all_to_all(wanted, CTX, split_axis=0, concat_axis=0, tiled=True)
    own_x = blocks // SIZE_X
    row_codes = lax.dynamic_slice(
        codes.reshape(SIZE_X, SIZE_Y, CORES, 128),
        (0, my_y, 0, my_x * own_x),
        (SIZE_X, 1, CORES, own_x),
    ).reshape(-1)
    peers = SIZE_X * CORES

    row_shape = (SIZE_X, CORES, own_x, rows // CORES, width)

    def along_row(tiles):
        tiles = tiles.reshape(peers, own_x, rows // CORES, width)
        received = lax.all_to_all(tiles, ("x", "core"), split_axis=0, concat_axis=0, tiled=True)
        return received.reshape(row_shape)

    early = count - 1
    far_keys = along_row(pack(row_codes, column, 0, own_x, width, *grads[1:early]))
    packed_values = pack(row_codes, column, 1, own_x, width, *grads[early:])
    far_values = along_row(gate(packed_values, far_keys[0, 0, 0, :16]))

    by_head = pl.BlockSpec((rows, width), lambda h, *_: (0, h))
    all_far = pl.BlockSpec(row_shape, lambda h, *_: (0, 0, 0, 0, 0))
    far = [
        pl.BlockSpec(
            (1, CORES, 1, rows // CORES, width),
            lambda h, sel, *_, j=j: (sel[h * picks + j] // own_x, 0, sel[h * picks + j] % own_x, 0, 0),
        )
        for j in range(picks)
    ]
    shares = [pl.BlockSpec((share_rows, width), lambda h, *_: (0, h))] * count
    by_stat = pl.BlockSpec((1, 1, rows), lambda h, *_: (h, 0, 0))
    near_shape = jax.ShapeDtypeStruct(queries.shape, jnp.bfloat16)
    far_shape = jax.ShapeDtypeStruct(row_shape, jnp.bfloat16)
    stat_shape = jax.ShapeDtypeStruct((heads, 1, rows), jnp.float32)
    scratch = [
        pltpu.VMEM((1, rows), jnp.int32),
        pltpu.VMEM((picks + 1, rows, rows), jnp.float32),
        pltpu.VMEM((rows, width), jnp.bfloat16),
    ]
    tile_flops = 2 * rows * rows * width * (picks + 1) * heads
    value_grad, far_value_grads, top, inverse = pl.pallas_call(
        value_grad_kernel,
        out_shape=(near_shape, far_shape, stat_shape, stat_shape),
        grid_spec=pltpu.PrefetchScalarGridSpec(
            num_scalar_prefetch=3,
            grid=(heads,),
            in_specs=[by_head, by_head, *far, *shares],
            out_specs=[by_head, all_far, by_stat, by_stat],
            scratch_shapes=scratch,
        ),
        compiler_params=pltpu.CompilerParams(vmem_limit_bytes=58 * MIB),
        cost_estimate=pl.CostEstimate(
            flops=2 * tile_flops, bytes_accessed=8 << 20, transcendentals=heads * 4 * rows * rows
        ),
    )(flat, doc_lengths, base, queries, keys, *[far_keys] * picks, *grads)
    value_terms = along_row(gate(far_value_grads, far_values[0, 0, 0, :16]))
    value_sums = row_sum(row_codes, value_terms.reshape(peers, *row_shape[2:]), heads)
    context_value_grad = lax.psum_scatter(value_sums, "y", scatter_dimension=0, tiled=True)

    attended, query_grad, key_grad, far_key_grads = pl.pallas_call(
        other_grads_kernel,
        out_shape=(near_shape, near_shape, near_shape, far_shape),
        grid_spec=pltpu.PrefetchScalarGridSpec(
            num_scalar_prefetch=3,
            grid=(heads,),
            in_specs=[by_head, by_head, by_head, *far, *far, by_stat, by_stat, *shares],
            out_specs=[by_head, by_head, by_head, all_far],
            scratch_shapes=scratch,
        ),
        compiler_params=pltpu.CompilerParams(vmem_limit_bytes=58 * MIB),
        cost_estimate=pl.CostEstimate(
            flops=5 * tile_flops, bytes_accessed=8 << 20, transcendentals=heads * 4 * rows * rows
        ),
    )(
        flat, doc_lengths, base, queries, keys, values,
        *[far_keys] * picks, *[far_values] * picks, top, inverse, *grads,
    )
    output_parts = shifted(
        [
            lax.dynamic_slice_in_dim(attended, lax.rem(me + d, count) * share_rows, share_rows, 0)
            for d in range(count)
        ],
        count,
    )
    key_terms = along_row(gate(far_key_grads, value_terms[0, 0, 0, :16]))
    key_sums = row_sum(row_codes, key_terms.reshape(peers, *row_shape[2:]), heads, *output_parts[1:6])
    key_sums = lax.all_to_all(key_sums, "y", split_axis=0, concat_axis=0, tiled=True)
    key_sums = key_sums.reshape(SIZE_Y, piece_rows, heads * width).astype(jnp.float32)
    context_key_grad = jnp.sum(key_sums, axis=0).astype(jnp.bfloat16)

    output_rows = pl.pallas_call(
        assemble_kernel,
        out_shape=jax.ShapeDtypeStruct((share_rows, count * heads * width), jnp.bfloat16),
        in_specs=[pl.BlockSpec(memory_space=pltpu.SMEM)]
        + [pl.BlockSpec(memory_space=pltpu.VMEM)] * count,
        out_specs=pl.BlockSpec(memory_space=pltpu.VMEM),
    )(me.reshape(1), *output_parts)
    return output_rows, query_grad, key_grad, value_grad, context_key_grad, context_value_grad


def solution(mesh):
    devices = mesh.devices.reshape(SIZE_X, SIZE_Y, CORES, -1)
    split = P(CTX, "head")
    rows = P((*CTX, "head"), None)
    return jax.shard_map(
        on_device,
        mesh=Mesh(devices, (*CTX, "head")),
        in_specs=(split, split, split, rows, split, split, P("head", CTX, None), P()),
        out_specs=(rows, split, split, split, split, split),
        check_vma=False,
    )
```

```python
import functools

import jax
import jax.numpy as jnp
from jax import lax
from jax.experimental import pallas as pl
from jax.experimental.pallas import tpu as pltpu
from jax.sharding import Mesh
from jax.sharding import PartitionSpec as P

NT = (((1,), (1,)), ((), ()))
NN = (((1,), (0,)), ((), ()))
SIZE_X, SIZE_Y, CORES = 4, 8, 2
CTX = ("x", "y", "core")
MIB = 1024 * 1024


def dot(a, b, dims):
    return lax.dot_general(a, b, dims, preferred_element_type=jnp.float32)


def document_starts(lens_ref, base_ref, rows):
    position = base_ref[0] + lax.broadcasted_iota(jnp.int32, (1, rows), 1)

    def step(d, carry):
        total, start = carry
        total = total + lens_ref[d]
        return total, jnp.maximum(start, jnp.where(total <= position, total, 0))

    _, start = lax.fori_loop(
        0, lens_ref.shape[0], step, (jnp.int32(0), jnp.zeros((1, rows), jnp.int32))
    )
    return start - base_ref[0]


def masked(scores, start):
    key_at = lax.broadcasted_iota(jnp.int32, scores.shape, 0)
    query_at = lax.broadcasted_iota(jnp.int32, scores.shape, 1)
    return jnp.where((key_at <= query_at) & (key_at >= start), scores, -jnp.inf)


def pack_kernel(sections, codes_ref, *refs):
    out_ref = refs[-1]
    count, rows, width = out_ref.shape
    first = pl.program_id(0) * count
    rows = rows // sections
    for j in range(count):
        column = pl.multiple_of(jnp.maximum(codes_ref[first + j], 0) * width, width)
        for i, section in enumerate(refs[:sections]):
            start = (j * rows) % section.shape[0]
            out_ref[j, i * rows : (i + 1) * rows] = section[
                start : start + rows, pl.ds(column, width)
            ]


def in_token_order(me, shares, out_ref):
    count = len(shares)
    rows = shares[0].shape[0]
    for distance, share in enumerate(shares):
        source = lax.rem(me + count - distance, count)
        out_ref[pl.ds(pl.multiple_of(source * rows, rows), rows), :] = share[...]


def key_tile(top, bottom):
    pieces = top.shape[1]
    order = [p * CORES + c for c in range(CORES) for p in range(pieces // CORES)]
    return jnp.concatenate([top[0, i] for i in order] + [bottom[0, c, 0] for c in range(CORES)], axis=0)


def value_tile(ref):
    rows = ref.shape[3] // 2
    return jnp.concatenate(
        [ref[0, c, 0, i * rows : (i + 1) * rows] for i in range(2) for c in range(CORES)], axis=0
    )


def store_halves(out_ref, block, part):
    own_x, rows = out_ref.shape[2:4]
    half = rows // 4
    for c in range(CORES):
        for p in range(2):
            for i in range(2):
                at = i * CORES * 2 * half + (c * 2 + p) * half
                to = (p * 2 + i) * half
                out_ref[block // own_x, c, lax.rem(block, own_x), to : to + half] = part[
                    at : at + half
                ]


def assemble_kernel(me_ref, *refs):
    *shares, out_ref = refs
    count = len(shares)
    width = shares[0].shape[1]
    for distance, share in enumerate(shares):
        source = lax.rem(me_ref[0] + count - distance, count)
        out_ref[:, pl.ds(pl.multiple_of(source * width, width), width)] = share[...]


def gate_kernel(kept_ref, after_ref, out_ref):
    pass


def value_grad_kernel(
    sel_ref, lens_ref, base_ref, q_ref, k_ref, *refs,
):
    far_k, refs = list(zip(refs[:3], refs[3:6])), refs[6:]
    *shares, near_ref, far_ref, top_ref, inverse_ref, start_ref, scores_ref, g_ref = refs
    head = pl.program_id(0)
    rows, width = q_ref.shape
    picks = scores_ref.shape[0] - 1
    scale = width ** (-0.5)

    @pl.when(head == 0)
    def _():
        start_ref[...] = document_starts(lens_ref, base_ref, rows)

    q = q_ref[...]
    near = masked(dot(k_ref[...], q, NT), start_ref[...])
    scores_ref[0] = near
    top = jnp.max(near, axis=0, keepdims=True)
    for j in range(picks):
        far = dot(key_tile(*far_k[j]), q, NT)
        scores_ref[j + 1] = far
        top = jnp.maximum(top, jnp.max(far, axis=0, keepdims=True))
    total = jnp.zeros((1, rows), jnp.float32)
    for j in range(picks + 1):
        lifted = jnp.exp((scores_ref[j] - top) * scale)
        scores_ref[j] = lifted
        total = total + jnp.sum(lifted, axis=0, keepdims=True)
    inverse = 1.0 / total
    top_ref[0] = top
    inverse_ref[0] = inverse
    in_token_order(base_ref[1], shares, g_ref)
    g = g_ref[...]
    for j in range(picks + 1):
        low = (scores_ref[j] * inverse).astype(jnp.bfloat16)
        part = dot(low, g, NN).astype(jnp.bfloat16)
        if j == 0:
            near_ref[...] = part
        else:
            store_halves(far_ref, sel_ref[head * picks + j - 1], part)


def other_grads_kernel(
    sel_ref, lens_ref, base_ref, q_ref, k_ref, v_ref,
    *refs,
):
    far_k, far_v, (top_ref, inverse_ref) = list(zip(refs[:3], refs[3:6])), refs[6:9], refs[9:11]
    *shares, attended_ref, query_ref, near_ref, far_ref, start_ref, weights_ref, g_ref = refs[11:]
    head = pl.program_id(0)
    rows, width = q_ref.shape
    picks = weights_ref.shape[0] - 1
    scale = width ** (-0.5)

    @pl.when(head == 0)
    def _():
        start_ref[...] = document_starts(lens_ref, base_ref, rows)

    def keys_of(j):
        return k_ref[...] if j == 0 else key_tile(*far_k[j - 1])

    def values_of(j):
        return v_ref[...] if j == 0 else value_tile(far_v[j - 1])

    in_token_order(base_ref[1], shares, g_ref)
    q = q_ref[...]
    g = g_ref[...]
    top = top_ref[0]
    inverse = inverse_ref[0]
    attended = jnp.zeros((width, rows), jnp.float32)
    for j in range(picks + 1):
        scores = dot(keys_of(j), q, NT)
        if j == 0:
            scores = masked(scores, start_ref[...])
        weights = jnp.exp((scores - top) * scale) * inverse
        weights_ref[j] = weights
        attended = attended + dot(values_of(j).T, weights.astype(jnp.bfloat16), NN)
    attended = attended.astype(jnp.bfloat16)
    attended_ref[...] = attended.T
    delta = jnp.sum(
        g.T.astype(jnp.float32) * attended.astype(jnp.float32), axis=0, keepdims=True
    )
    query_grad = jnp.zeros((width, rows), jnp.float32)
    for j in range(picks + 1):
        weight_grads = dot(values_of(j), g, NT)
        score_grads = (weights_ref[j] * (weight_grads - delta) * scale).astype(jnp.bfloat16)
        part = dot(score_grads, q, NN).astype(jnp.bfloat16)
        if j == 0:
            near_ref[...] = part
        else:
            store_halves(far_ref, sel_ref[head * picks + j - 1], part)
        query_grad = query_grad + dot(keys_of(j).T, score_grads, NN)
    query_ref[...] = query_grad.astype(jnp.bfloat16).T


def pack(codes, context, rows, columns, sections, groups, width, *after):
    slots = codes.shape[0]
    steps = 4
    slot_rows = rows // groups * len(sections)
    return pl.pallas_call(
        functools.partial(pack_kernel, len(sections)),
        out_shape=jax.ShapeDtypeStruct((slots, slot_rows, width), context.dtype),
        grid_spec=pltpu.PrefetchScalarGridSpec(
            num_scalar_prefetch=1,
            grid=(steps,),
            in_specs=[pl.BlockSpec((rows, columns), lambda i, *_, at=at: (0, at)) for at in sections]
            + [pl.BlockSpec(memory_space=pl.ANY)] * len(after),
            out_specs=pl.BlockSpec((slots // steps, slot_rows, width), lambda i, *_: (i, 0, 0)),
        ),
        compiler_params=pltpu.CompilerParams(vmem_limit_bytes=60 * MIB),
    )(codes, *[context] * len(sections), *after)


def row_sum_kernel(codes_ref, terms_ref, *refs):
    out_ref, total_ref = refs[-2:]
    block = pl.program_id(0)
    sources, _, rows, width = terms_ref.shape
    heads = total_ref.shape[0] - 1
    total_ref[...] = jnp.zeros_like(total_ref)

    def step(s, carry):
        code = codes_ref[s * pl.num_programs(0) + block]
        slot = jnp.where(code >= 0, code, heads)
        total_ref[slot] += terms_ref[s, 0].astype(jnp.float32)
        return carry

    lax.fori_loop(0, sources, step, 0)
    for h in range(heads):
        out_ref[:, h * width : (h + 1) * width] = total_ref[h].astype(out_ref.dtype)


def row_sum(codes, terms, heads, *after):
    sources, blocks, rows, width = terms.shape
    return pl.pallas_call(
        row_sum_kernel,
        out_shape=jax.ShapeDtypeStruct((blocks * rows, heads * width), terms.dtype),
        grid_spec=pltpu.PrefetchScalarGridSpec(
            num_scalar_prefetch=1,
            grid=(blocks,),
            in_specs=[pl.BlockSpec((sources, 1, rows, width), lambda i, *_: (0, i, 0, 0))]
            + [pl.BlockSpec(memory_space=pl.ANY)] * len(after),
            out_specs=pl.BlockSpec((rows, heads * width), lambda i, *_: (i, 0)),
            scratch_shapes=[pltpu.VMEM((heads + 1, rows, width), jnp.float32)],
        ),
        compiler_params=pltpu.CompilerParams(vmem_limit_bytes=6 * MIB),
    )(codes, terms, *after)


def shifted(parts, count):
    return [parts[0]] + [
        lax.ppermute(parts[d], "head", [(i, (i + d) % count) for i in range(count)])
        for d in range(1, count)
    ]


def gate(kept, after):
    return pl.pallas_call(
        gate_kernel,
        out_shape=jax.ShapeDtypeStruct(kept.shape, kept.dtype),
        in_specs=[pl.BlockSpec(memory_space=pl.ANY)] * 2,
        out_specs=pl.BlockSpec(memory_space=pl.ANY),
        input_output_aliases={0: 0},
    )(kept, after)


def on_device(queries, keys, values, out_grad, context_keys, context_values, selected, doc_lengths):
    heads, _, picks = selected.shape
    rows = queries.shape[0]
    width = queries.shape[1] // heads
    piece_rows = context_keys.shape[0]
    pieces = rows // piece_rows
    owners = lax.axis_size(CTX)
    blocks = owners // pieces
    my_x, my_y = lax.axis_index("x"), lax.axis_index("y")
    my_piece = lax.axis_index(CTX).astype(jnp.int32)
    half = piece_rows // 2
    columns = heads * width
    column = lax.all_gather(
        jnp.concatenate([context_keys[half:], context_values[:half], context_values[half:]], axis=1),
        "y",
        axis=0,
        tiled=True,
    )
    count = lax.axis_size("head")
    me = lax.axis_index("head").astype(jnp.int32)
    share_rows = rows // count
    base = jnp.stack([my_piece * rows, me])
    flat = selected.reshape(-1)

    head_of = jnp.arange(heads * picks, dtype=jnp.int32) // picks
    hits = flat[None, :] == jnp.arange(blocks, dtype=jnp.int32)[:, None]
    wanted = jnp.max(jnp.where(hits, head_of[None, :], -1), axis=1)
    wanted = jnp.broadcast_to(jnp.pad(wanted, (0, 128 - blocks)), (owners, 128))
    codes = lax.all_to_all(wanted, CTX, split_axis=0, concat_axis=0, tiled=True)
    settled = codes[0, 127]
    grads = shifted(
        [
            lax.dynamic_slice_in_dim(out_grad, lax.rem(me + d, count) * columns + settled, columns, 1)
            for d in range(count)
        ],
        count,
    )
    own_x = blocks // SIZE_X
    piece_codes = lax.dynamic_slice_in_dim(codes, my_piece // pieces, 1, 1)[:, 0]
    row_codes = lax.dynamic_slice(
        codes.reshape(SIZE_X, SIZE_Y, CORES, 128),
        (0, my_y, 0, my_x * own_x),
        (SIZE_X, 1, CORES, own_x),
    ).reshape(-1)
    peers = SIZE_X * CORES

    row_shape = (SIZE_X, CORES, own_x, rows // CORES, width)

    def along_row(tiles):
        tiles = tiles.reshape(peers, own_x, -1, width)
        received = lax.all_to_all(tiles, ("x", "core"), split_axis=0, concat_axis=0, tiled=True)
        return received.reshape(*row_shape[:3], -1, width)

    early = count - 1
    top_keys = lax.all_to_all(
        pack(piece_codes, context_keys, half, columns, [0], 1, width),
        CTX,
        split_axis=0,
        concat_axis=0,
        tiled=True,
    ).reshape(blocks, pieces, half, width)
    column_rows = SIZE_Y * half
    packed_keys = pack(row_codes, column, column_rows, columns, [0], own_x, width, *grads[1:early])
    bottom_keys = along_row(gate(packed_keys, top_keys[0, 0, :16]))
    packed_values = pack(row_codes, column, column_rows, columns, [1, 2], own_x, width, *grads[early:])
    far_values = along_row(gate(packed_values, bottom_keys[0, 0, 0, :16]))

    by_head = pl.BlockSpec((rows, width), lambda h, *_: (0, h))
    all_far = pl.BlockSpec(row_shape, lambda h, *_: (0, 0, 0, 0, 0))
    far_top = [
        pl.BlockSpec((1, pieces, half, width), lambda h, sel, *_, j=j: (sel[h * picks + j], 0, 0, 0))
        for j in range(picks)
    ]

    def by_row(block_rows):
        return [
            pl.BlockSpec(
                (1, CORES, 1, block_rows, width),
                lambda h, sel, *_, j=j: (
                    sel[h * picks + j] // own_x, 0, sel[h * picks + j] % own_x, 0, 0
                ),
            )
            for j in range(picks)
        ]

    far_bottom, far = by_row(2 * half), by_row(rows // CORES)
    shares = [pl.BlockSpec((share_rows, width), lambda h, *_: (0, h))] * count
    by_stat = pl.BlockSpec((1, 1, rows), lambda h, *_: (h, 0, 0))
    near_shape = jax.ShapeDtypeStruct(queries.shape, jnp.bfloat16)
    far_shape = jax.ShapeDtypeStruct(row_shape, jnp.bfloat16)
    stat_shape = jax.ShapeDtypeStruct((heads, 1, rows), jnp.float32)
    scratch = [
        pltpu.VMEM((1, rows), jnp.int32),
        pltpu.VMEM((picks + 1, rows, rows), jnp.float32),
        pltpu.VMEM((rows, width), jnp.bfloat16),
    ]
    tile_flops = 2 * rows * rows * width * (picks + 1) * heads
    value_grad, far_value_grads, top, inverse = pl.pallas_call(
        value_grad_kernel,
        out_shape=(near_shape, far_shape, stat_shape, stat_shape),
        grid_spec=pltpu.PrefetchScalarGridSpec(
            num_scalar_prefetch=3,
            grid=(heads,),
            in_specs=[by_head, by_head, *far_top, *far_bottom, *shares],
            out_specs=[by_head, all_far, by_stat, by_stat],
            scratch_shapes=scratch,
        ),
        compiler_params=pltpu.CompilerParams(vmem_limit_bytes=58 * MIB),
        cost_estimate=pl.CostEstimate(
            flops=2 * tile_flops, bytes_accessed=8 << 20, transcendentals=heads * 4 * rows * rows
        ),
    )(flat, doc_lengths, base, queries, keys, *[top_keys] * picks, *[bottom_keys] * picks, *grads)
    value_terms = along_row(gate(far_value_grads, far_values[0, 0, 0, :16]))
    value_sums = row_sum(row_codes, value_terms.reshape(peers, *row_shape[2:]), heads)
    context_value_grad = lax.psum_scatter(value_sums, "y", scatter_dimension=0, tiled=True)

    attended, query_grad, key_grad, far_key_grads = pl.pallas_call(
        other_grads_kernel,
        out_shape=(near_shape, near_shape, near_shape, far_shape),
        grid_spec=pltpu.PrefetchScalarGridSpec(
            num_scalar_prefetch=3,
            grid=(heads,),
            in_specs=[
                by_head, by_head, by_head, *far_top, *far_bottom, *far, by_stat, by_stat, *shares
            ],
            out_specs=[by_head, by_head, by_head, all_far],
            scratch_shapes=scratch,
        ),
        compiler_params=pltpu.CompilerParams(vmem_limit_bytes=58 * MIB),
        cost_estimate=pl.CostEstimate(
            flops=5 * tile_flops, bytes_accessed=8 << 20, transcendentals=heads * 4 * rows * rows
        ),
    )(
        flat, doc_lengths, base, queries, keys, values,
        *[top_keys] * picks, *[bottom_keys] * picks, *[far_values] * picks, top, inverse, *grads,
    )
    output_parts = shifted(
        [
            lax.dynamic_slice_in_dim(attended, lax.rem(me + d, count) * share_rows, share_rows, 0)
            for d in range(count)
        ],
        count,
    )
    key_terms = along_row(gate(far_key_grads, value_terms[0, 0, 0, :16]))
    key_sums = row_sum(row_codes, key_terms.reshape(peers, *row_shape[2:]), heads, *output_parts[1:6])
    key_sums = lax.all_to_all(key_sums, "y", split_axis=0, concat_axis=0, tiled=True)
    key_sums = key_sums.reshape(SIZE_Y, piece_rows, heads * width).astype(jnp.float32)
    context_key_grad = jnp.sum(key_sums, axis=0).astype(jnp.bfloat16)

    output_rows = pl.pallas_call(
        assemble_kernel,
        out_shape=jax.ShapeDtypeStruct((share_rows, count * heads * width), jnp.bfloat16),
        in_specs=[pl.BlockSpec(memory_space=pltpu.SMEM)]
        + [pl.BlockSpec(memory_space=pltpu.VMEM)] * count,
        out_specs=pl.BlockSpec(memory_space=pltpu.VMEM),
    )(me.reshape(1), *output_parts)
    return output_rows, query_grad, key_grad, value_grad, context_key_grad, context_value_grad


def solution(mesh):
    devices = mesh.devices.reshape(SIZE_X, SIZE_Y, CORES, -1)
    split = P(CTX, "head")
    rows = P((*CTX, "head"), None)
    return jax.shard_map(
        on_device,
        mesh=Mesh(devices, (*CTX, "head")),
        in_specs=(split, split, split, rows, split, split, P("head", CTX, None), P()),
        out_specs=(rows, split, split, split, split, split),
        check_vma=False,
    )
```

```python
import jax
import jax.numpy as jnp
from jax import lax
from jax.experimental import pallas as pl
from jax.experimental.pallas import tpu as pltpu
from jax.sharding import Mesh
from jax.sharding import PartitionSpec as P

NT = (((1,), (1,)), ((), ()))
NN = (((1,), (0,)), ((), ()))
SIZE_X, SIZE_Y, CORES = 4, 8, 2
CTX = ("x", "y", "core")
MIB = 1024 * 1024


def dot(a, b, dims):
    return lax.dot_general(a, b, dims, preferred_element_type=jnp.float32)


def document_starts(lens_ref, base_ref, rows):
    position = base_ref[0] + lax.broadcasted_iota(jnp.int32, (1, rows), 1)

    def step(d, carry):
        total, start = carry
        total = total + lens_ref[d]
        return total, jnp.maximum(start, jnp.where(total <= position, total, 0))

    _, start = lax.fori_loop(
        0, lens_ref.shape[0], step, (jnp.int32(0), jnp.zeros((1, rows), jnp.int32))
    )
    return start - base_ref[0]


def masked(scores, start):
    key_at = lax.broadcasted_iota(jnp.int32, scores.shape, 0)
    query_at = lax.broadcasted_iota(jnp.int32, scores.shape, 1)
    return jnp.where((key_at <= query_at) & (key_at >= start), scores, -jnp.inf)


def pack_kernel(codes_ref, context_ref, *refs):
    out_ref = refs[-1]
    count, out_rows, width = out_ref.shape
    pieces, _, rows, _ = context_ref.shape
    first = pl.program_id(0) * count
    each = out_rows // rows
    for j in range(count):
        column = pl.multiple_of(jnp.maximum(codes_ref[first + j], 0) * width, width)
        for p in range(each):
            out_ref[j, p * rows : (p + 1) * rows] = context_ref[
                (j * each + p) % pieces, 0, :, pl.ds(column, width)
            ]


def in_token_order(me, shares, out_ref):
    count = len(shares)
    rows = shares[0].shape[0]
    for distance, share in enumerate(shares):
        source = lax.rem(me + count - distance, count)
        out_ref[pl.ds(pl.multiple_of(source * rows, rows), rows), :] = share[...]


def tile_of(ref):
    return ref[...].reshape(-1, ref.shape[-1])


def store_halves(out_ref, block, part):
    own_x, rows = out_ref.shape[2:4]
    for c in range(CORES):
        out_ref[block // own_x, c, lax.rem(block, own_x)] = part[c * rows : (c + 1) * rows]


def assemble_kernel(me_ref, *refs):
    *shares, out_ref = refs
    count = len(shares)
    width = shares[0].shape[1]
    for distance, share in enumerate(shares):
        source = lax.rem(me_ref[0] + count - distance, count)
        out_ref[:, pl.ds(pl.multiple_of(source * width, width), width)] = share[...]


def gate_kernel(kept_ref, after_ref, out_ref):
    pass


def value_grad_kernel(
    sel_ref, lens_ref, base_ref, q_ref, k_ref, k1_ref, k2_ref, k3_ref, *refs,
):
    *shares, near_ref, far_ref, top_ref, inverse_ref, start_ref, scores_ref, g_ref = refs
    far_k = (k1_ref, k2_ref, k3_ref)
    head = pl.program_id(0)
    rows, width = q_ref.shape
    picks = scores_ref.shape[0] - 1
    scale = width ** (-0.5)

    @pl.when(head == 0)
    def _():
        start_ref[...] = document_starts(lens_ref, base_ref, rows)

    q = q_ref[...]
    near = masked(dot(k_ref[...], q, NT), start_ref[...])
    scores_ref[0] = near
    top = jnp.max(near, axis=0, keepdims=True)
    for j in range(picks):
        far = dot(tile_of(far_k[j]), q, NT)
        scores_ref[j + 1] = far
        top = jnp.maximum(top, jnp.max(far, axis=0, keepdims=True))
    total = jnp.zeros((1, rows), jnp.float32)
    for j in range(picks + 1):
        lifted = jnp.exp((scores_ref[j] - top) * scale)
        scores_ref[j] = lifted
        total = total + jnp.sum(lifted, axis=0, keepdims=True)
    inverse = 1.0 / total
    top_ref[0] = top
    inverse_ref[0] = inverse
    in_token_order(base_ref[1], shares, g_ref)
    g = g_ref[...]
    for j in range(picks + 1):
        low = (scores_ref[j] * inverse).astype(jnp.bfloat16)
        part = dot(low, g, NN).astype(jnp.bfloat16)
        if j == 0:
            near_ref[...] = part
        else:
            store_halves(far_ref, sel_ref[head * picks + j - 1], part)


def other_grads_kernel(
    sel_ref, lens_ref, base_ref, q_ref, k_ref, v_ref,
    k1_ref, k2_ref, k3_ref, v1_ref, v2_ref, v3_ref, top_ref, inverse_ref, *refs,
):
    *shares, attended_ref, query_ref, near_ref, far_ref, start_ref, weights_ref, g_ref = refs
    far_k, far_v = (k1_ref, k2_ref, k3_ref), (v1_ref, v2_ref, v3_ref)
    head = pl.program_id(0)
    rows, width = q_ref.shape
    picks = weights_ref.shape[0] - 1
    scale = width ** (-0.5)

    @pl.when(head == 0)
    def _():
        start_ref[...] = document_starts(lens_ref, base_ref, rows)

    def keys_of(j):
        return k_ref[...] if j == 0 else tile_of(far_k[j - 1])

    def values_of(j):
        return v_ref[...] if j == 0 else tile_of(far_v[j - 1])

    in_token_order(base_ref[1], shares, g_ref)
    q = q_ref[...]
    g = g_ref[...]
    top = top_ref[0]
    inverse = inverse_ref[0]
    attended = jnp.zeros((width, rows), jnp.float32)
    for j in range(picks + 1):
        scores = dot(keys_of(j), q, NT)
        if j == 0:
            scores = masked(scores, start_ref[...])
        weights = jnp.exp((scores - top) * scale) * inverse
        weights_ref[j] = weights
        attended = attended + dot(values_of(j).T, weights.astype(jnp.bfloat16), NN)
    attended = attended.astype(jnp.bfloat16)
    attended_ref[...] = attended.T
    delta = jnp.sum(
        g.T.astype(jnp.float32) * attended.astype(jnp.float32), axis=0, keepdims=True
    )
    query_grad = jnp.zeros((width, rows), jnp.float32)
    for j in range(picks + 1):
        weight_grads = dot(values_of(j), g, NT)
        score_grads = (weights_ref[j] * (weight_grads - delta) * scale).astype(jnp.bfloat16)
        part = dot(score_grads, q, NN).astype(jnp.bfloat16)
        if j == 0:
            near_ref[...] = part
        else:
            store_halves(far_ref, sel_ref[head * picks + j - 1], part)
        query_grad = query_grad + dot(keys_of(j).T, score_grads, NN)
    query_ref[...] = query_grad.astype(jnp.bfloat16).T


def pack(codes, context, half, groups, width, *after):
    slots = codes.shape[0]
    pieces, _, rows, columns = context.shape
    slot_rows = pieces // groups * rows
    steps = 4
    return pl.pallas_call(
        pack_kernel,
        out_shape=jax.ShapeDtypeStruct((slots, slot_rows, width), context.dtype),
        grid_spec=pltpu.PrefetchScalarGridSpec(
            num_scalar_prefetch=1,
            grid=(steps,),
            in_specs=[pl.BlockSpec((pieces, 1, rows, columns), lambda i, *_: (0, half, 0, 0))]
            + [pl.BlockSpec(memory_space=pl.ANY)] * len(after),
            out_specs=pl.BlockSpec((slots // steps, slot_rows, width), lambda i, *_: (i, 0, 0)),
        ),
        compiler_params=pltpu.CompilerParams(vmem_limit_bytes=60 * MIB),
    )(codes, context, *after)


def row_sum_kernel(codes_ref, terms_ref, *refs):
    out_ref, total_ref = refs[-2:]
    block = pl.program_id(0)
    sources, _, rows, width = terms_ref.shape
    heads = total_ref.shape[0] - 1
    total_ref[...] = jnp.zeros_like(total_ref)

    def step(s, carry):
        code = codes_ref[s * pl.num_programs(0) + block]
        slot = jnp.where(code >= 0, code, heads)
        total_ref[slot] += terms_ref[s, 0].astype(jnp.float32)
        return carry

    lax.fori_loop(0, sources, step, 0)
    for h in range(heads):
        out_ref[:, h * width : (h + 1) * width] = total_ref[h].astype(out_ref.dtype)


def row_sum(codes, terms, heads, *after):
    sources, blocks, rows, width = terms.shape
    return pl.pallas_call(
        row_sum_kernel,
        out_shape=jax.ShapeDtypeStruct((blocks * rows, heads * width), terms.dtype),
        grid_spec=pltpu.PrefetchScalarGridSpec(
            num_scalar_prefetch=1,
            grid=(blocks,),
            in_specs=[pl.BlockSpec((sources, 1, rows, width), lambda i, *_: (0, i, 0, 0))]
            + [pl.BlockSpec(memory_space=pl.ANY)] * len(after),
            out_specs=pl.BlockSpec((rows, heads * width), lambda i, *_: (i, 0)),
            scratch_shapes=[pltpu.VMEM((heads + 1, rows, width), jnp.float32)],
        ),
        compiler_params=pltpu.CompilerParams(vmem_limit_bytes=6 * MIB),
    )(codes, terms, *after)


def shifted(parts, count):
    return [parts[0]] + [
        lax.ppermute(parts[d], "head", [(i, (i + d) % count) for i in range(count)])
        for d in range(1, count)
    ]


def gate(kept, after):
    return pl.pallas_call(
        gate_kernel,
        out_shape=jax.ShapeDtypeStruct(kept.shape, kept.dtype),
        in_specs=[pl.BlockSpec(memory_space=pl.ANY)] * 2,
        out_specs=pl.BlockSpec(memory_space=pl.ANY),
        input_output_aliases={0: 0},
    )(kept, after)


def on_device(queries, keys, values, out_grad, context_keys, context_values, selected, doc_lengths):
    heads, _, picks = selected.shape
    rows = queries.shape[0]
    width = queries.shape[1] // heads
    piece_rows = context_keys.shape[0]
    pieces = rows // piece_rows
    owners = lax.axis_size(CTX)
    blocks = owners // pieces
    my_x, my_y = lax.axis_index("x"), lax.axis_index("y")
    my_piece = lax.axis_index(CTX).astype(jnp.int32)
    column = lax.all_gather(jnp.stack([context_keys, context_values]), "y", axis=0)
    count = lax.axis_size("head")
    me = lax.axis_index("head").astype(jnp.int32)
    share_rows = rows // count
    grads = shifted(
        [
            lax.dynamic_slice_in_dim(
                out_grad, lax.rem(me + d, count) * heads * width, heads * width, 1
            )
            for d in range(count)
        ],
        count,
    )
    base = jnp.stack([my_piece * rows, me])
    flat = selected.reshape(-1)

    head_of = jnp.arange(heads * picks, dtype=jnp.int32) // picks
    hits = flat[None, :] == jnp.arange(blocks, dtype=jnp.int32)[:, None]
    wanted = jnp.max(jnp.where(hits, head_of[None, :], -1), axis=1)
    wanted = jnp.broadcast_to(jnp.pad(wanted, (0, 128 - blocks)), (owners, 128))
    codes = lax.all_to_all(wanted, CTX, split_axis=0, concat_axis=0, tiled=True)
    own_x = blocks // SIZE_X
    row_codes = lax.dynamic_slice(
        codes.reshape(SIZE_X, SIZE_Y, CORES, 128),
        (0, my_y, 0, my_x * own_x),
        (SIZE_X, 1, CORES, own_x),
    ).reshape(-1)
    peers = SIZE_X * CORES

    row_shape = (SIZE_X, CORES, own_x, rows // CORES, width)

    def along_row(tiles):
        tiles = tiles.reshape(peers, own_x, rows // CORES, width)
        received = lax.all_to_all(tiles, ("x", "core"), split_axis=0, concat_axis=0, tiled=True)
        return received.reshape(row_shape)

    early = count - 1
    far_keys = along_row(pack(row_codes, column, 0, own_x, width, *grads[1:early]))
    packed_values = pack(row_codes, column, 1, own_x, width, *grads[early:])
    far_values = along_row(gate(packed_values, far_keys[0, 0, 0, :16]))

    by_head = pl.BlockSpec((rows, width), lambda h, *_: (0, h))
    all_far = pl.BlockSpec(row_shape, lambda h, *_: (0, 0, 0, 0, 0))
    far = [
        pl.BlockSpec(
            (1, CORES, 1, rows // CORES, width),
            lambda h, sel, *_, j=j: (sel[h * picks + j] // own_x, 0, sel[h * picks + j] % own_x, 0, 0),
        )
        for j in range(picks)
    ]
    shares = [pl.BlockSpec((share_rows, width), lambda h, *_: (0, h))] * count
    by_stat = pl.BlockSpec((1, 1, rows), lambda h, *_: (h, 0, 0))
    near_shape = jax.ShapeDtypeStruct(queries.shape, jnp.bfloat16)
    far_shape = jax.ShapeDtypeStruct(row_shape, jnp.bfloat16)
    stat_shape = jax.ShapeDtypeStruct((heads, 1, rows), jnp.float32)
    scratch = [
        pltpu.VMEM((1, rows), jnp.int32),
        pltpu.VMEM((picks + 1, rows, rows), jnp.float32),
        pltpu.VMEM((rows, width), jnp.bfloat16),
    ]
    tile_flops = 2 * rows * rows * width * (picks + 1) * heads
    value_grad, far_value_grads, top, inverse = pl.pallas_call(
        value_grad_kernel,
        out_shape=(near_shape, far_shape, stat_shape, stat_shape),
        grid_spec=pltpu.PrefetchScalarGridSpec(
            num_scalar_prefetch=3,
            grid=(heads,),
            in_specs=[by_head, by_head, *far, *shares],
            out_specs=[by_head, all_far, by_stat, by_stat],
            scratch_shapes=scratch,
        ),
        compiler_params=pltpu.CompilerParams(vmem_limit_bytes=58 * MIB),
        cost_estimate=pl.CostEstimate(
            flops=2 * tile_flops, bytes_accessed=8 << 20, transcendentals=heads * 4 * rows * rows
        ),
    )(flat, doc_lengths, base, queries, keys, *[far_keys] * picks, *grads)
    value_terms = along_row(gate(far_value_grads, far_values[0, 0, 0, :16]))
    value_sums = row_sum(row_codes, value_terms.reshape(peers, *row_shape[2:]), heads)
    context_value_grad = lax.psum_scatter(value_sums, "y", scatter_dimension=0, tiled=True)

    attended, query_grad, key_grad, far_key_grads = pl.pallas_call(
        other_grads_kernel,
        out_shape=(near_shape, near_shape, near_shape, far_shape),
        grid_spec=pltpu.PrefetchScalarGridSpec(
            num_scalar_prefetch=3,
            grid=(heads,),
            in_specs=[by_head, by_head, by_head, *far, *far, by_stat, by_stat, *shares],
            out_specs=[by_head, by_head, by_head, all_far],
            scratch_shapes=scratch,
        ),
        compiler_params=pltpu.CompilerParams(vmem_limit_bytes=58 * MIB),
        cost_estimate=pl.CostEstimate(
            flops=5 * tile_flops, bytes_accessed=8 << 20, transcendentals=heads * 4 * rows * rows
        ),
    )(
        flat, doc_lengths, base, queries, keys, values,
        *[far_keys] * picks, *[far_values] * picks, top, inverse, *grads,
    )
    output_parts = shifted(
        [
            lax.dynamic_slice_in_dim(attended, lax.rem(me + d, count) * share_rows, share_rows, 0)
            for d in range(count)
        ],
        count,
    )
    key_terms = along_row(gate(far_key_grads, value_terms[0, 0, 0, :16]))
    key_sums = row_sum(row_codes, key_terms.reshape(peers, *row_shape[2:]), heads, *output_parts[1:4])
    key_sums = lax.all_to_all(key_sums, "y", split_axis=0, concat_axis=0, tiled=True)
    key_sums = key_sums.reshape(SIZE_Y, piece_rows, heads * width).astype(jnp.float32)
    context_key_grad = jnp.sum(key_sums, axis=0).astype(jnp.bfloat16)

    output_rows = pl.pallas_call(
        assemble_kernel,
        out_shape=jax.ShapeDtypeStruct((share_rows, count * heads * width), jnp.bfloat16),
        in_specs=[pl.BlockSpec(memory_space=pltpu.SMEM)]
        + [pl.BlockSpec(memory_space=pltpu.VMEM)] * count,
        out_specs=pl.BlockSpec(memory_space=pltpu.VMEM),
    )(me.reshape(1), *output_parts)
    return output_rows, query_grad, key_grad, value_grad, context_key_grad, context_value_grad


def solution(mesh):
    devices = mesh.devices.reshape(SIZE_X, SIZE_Y, CORES, -1)
    split = P(CTX, "head")
    rows = P((*CTX, "head"), None)
    return jax.shard_map(
        on_device,
        mesh=Mesh(devices, (*CTX, "head")),
        in_specs=(split, split, split, rows, split, split, P("head", CTX, None), P()),
        out_specs=(rows, split, split, split, split, split),
        check_vma=False,
    )
```
